128 devices in a mesh: row: 32 (over x, z, core), col: 4 (over y).
Axes of the slice: x: 4, y: 4, z: 4, core: 2. Of those that a mesh axis runs over, the one named last changes fastest.
Arguments:
- influence: float32 [131072, 1024], P('row', 'col'), may hold values from -320 to 320, as said below
Outputs:
- factored: float32 [131072, 1024], P('row', 'col')
- upper: float32 [512, 1024], P(None, 'col')
The draws below stay inside these ranges and needn't reach their ends.
Inputs may be any that keep to these rules, and one draw needn't show every extreme that they name: `influence`: real-valued samples.
All inputs are finite; a program needn't handle non-finite values.
Results may differ from the reference program's by a relative error of at most 0.000068.
Values sent between devices are 32-bit elements; how exact they have to be, the bound alone decides.
A program may use at most 128 MiB of HBM per device.

```python
import math
import jax
import jax.numpy as jnp
from jax import lax

PANEL = 256
ROWS = 131072
COLUMNS = 1024


def blend_columns(noise):
    mixed = noise + 0.9 * jnp.roll(noise, 1, axis=1) + 0.5 * jnp.roll(noise, 2, axis=1)
    return mixed * (1.0 / math.sqrt(2.06))


def draw_influence(key, part):
    keys = jax.random.split(key, 4)
    shared = jnp.clip(jax.random.normal(keys[0], (ROWS, PANEL), jnp.float32), -5.0, 5.0)
    noise = jnp.clip(jax.random.normal(keys[1], (ROWS, COLUMNS), jnp.float32), -4.5, 4.5)
    row_low = 0.25
    row_high = 2.5
    row_scale = jnp.exp(jax.random.uniform(keys[2], (ROWS, 1), jnp.float32, math.log(row_low), math.log(row_high)))
    ramp = 1.0 + 2.0 * jnp.arange(ROWS, dtype=jnp.float32)[:, None] / ROWS
    col_scale = jnp.exp(jax.random.uniform(keys[3], (1, COLUMNS), jnp.float32, math.log(0.32), math.log(3.2)))
    values = jnp.tile(shared, (1, COLUMNS // PANEL)) + blend_columns(noise)
    return (row_scale * ramp * col_scale * values).astype(jnp.float32)


def setup_inputs(seed: int = 0) -> dict:
    key_list = jax.random.split(jax.random.key(seed), 2)
    influence = draw_influence(jax.random.fold_in(key_list[1], 71), 0)
    return {"influence": influence}


def factor_panel(block):
    gram = jnp.dot(block.T, block, precision=lax.Precision.HIGHEST) / ROWS
    lower = jnp.linalg.cholesky(gram)
    eye = jnp.eye(PANEL, dtype=jnp.float32)
    inverse = lax.linalg.triangular_solve(lower, eye, left_side=True, lower=True)
    basis = jnp.dot(block, inverse.T, precision=lax.Precision.HIGHEST)
    return (lower, basis)

def reference(influence):
    first = influence[:, :PANEL]
    rest = influence[:, PANEL:]
    lower1, basis1 = factor_panel(first)
    coeff1 = jnp.dot(basis1.T, rest, precision=lax.Precision.HIGHEST) / ROWS
    rest1 = rest - jnp.dot(basis1, coeff1, precision=lax.Precision.HIGHEST)
    second = rest1[:, :PANEL]
    tail = rest1[:, PANEL:]
    lower2, basis2 = factor_panel(second)
    coeff2 = jnp.dot(basis2.T, tail, precision=lax.Precision.HIGHEST) / ROWS
    tail2 = tail - jnp.dot(basis2, coeff2, precision=lax.Precision.HIGHEST)
    factored = jnp.concatenate([basis1, basis2, tail2], axis=1)
    top_rows = jnp.concatenate([lower1.T, coeff1], axis=1)
    bottom_rows = jnp.concatenate([jnp.zeros((PANEL, PANEL), jnp.float32), lower2.T, coeff2], axis=1)
    upper = jnp.concatenate([top_rows, bottom_rows], axis=0)
    return (factored, upper)
```

```python
import functools

import jax
import jax.numpy as jnp
from jax import lax
from jax.experimental import pallas as pl
from jax.experimental.pallas import tpu as pltpu
from jax.sharding import PartitionSpec as P

MESH = pl.DeviceIdType.MESH
F32 = jnp.float32
PANEL = 256
HALF = 128
ROWS = 4096
CHUNK = 128
PIECES = ROWS // CHUNK
EARLY = PIECES // 2
GROUP = 512
APPLY = 256


def mm(a, b, ca=1, cb=0):
    return lax.dot_general(
        a, b, (((ca,), (cb,)), ((), ())),
        precision=lax.Precision.HIGHEST, preferred_element_type=F32,
    )


def spread(v):
    return jnp.broadcast_to(v, (8, HALF))


def eliminate(square, u_ref, li_ref, off, nb=4):
    sub = lax.broadcasted_iota(jnp.int32, (8, HALF), 0)
    lane = lax.broadcasted_iota(jnp.int32, (8, HALF), 1)
    zero = jnp.zeros((8, HALF), F32)
    tiles = HALF // 8
    left = tuple(square[8 * i : 8 * i + 8, :] for i in range(tiles))
    right = tuple(jnp.where(lane == sub + 8 * i, 1.0, 0.0).astype(F32) for i in range(tiles))

    def eight(left, right, q):
        w = [spread(left[0][:, 8 * q + m : 8 * q + m + 1]) for m in range(8)] + [left[0], right[0]]
        rows = [zero, zero]
        for j in range(0, 8, 2):
            pivot = (sub == j) | (sub == j + 1)
            p00, p01, p11 = spread(w[j][j : j + 1]), spread(w[j][j + 1 : j + 2]), spread(w[j + 1][j + 1 : j + 2])
            rd = 1.0 / (p00 * p11 - p01 * p01)
            i00, i01, i11 = p11 * rd, p01 * rd, p00 * rd
            u, v = jnp.where(pivot, 0.0, w[j]), jnp.where(pivot, 0.0, w[j + 1])
            s0 = lax.rsqrt(p00)
            m0 = p01 * (s0 * s0)
            s1 = lax.rsqrt(p11 - m0 * p01)
            for t in list(range(j + 2, 8)) + [8, 9]:
                r0, r1 = spread(w[t][j : j + 1]), spread(w[t][j + 1 : j + 2])
                a, b = r0 * i00 - r1 * i01, r1 * i11 - r0 * i01
                if t >= 8:
                    rows[t - 8] = jnp.where(
                        sub == j, r0 * s0, jnp.where(sub == j + 1, (r1 - m0 * r0) * s1, rows[t - 8])
                    )
                w[t] = jnp.where(sub == j, a, jnp.where(sub == j + 1, b, w[t] - (u * a + v * b)))
        ql = [spread(w[8][m : m + 1]) for m in range(8)]
        qr = [spread(w[9][m : m + 1]) for m in range(8)]

        def total(c, q):
            t = [c[m] * q[m] for m in range(8)]
            return ((t[0] + t[1]) + (t[2] + t[3])) + ((t[4] + t[5]) + (t[6] + t[7]))

        for i in range(1, tiles):
            c = [spread(left[i][:, 8 * q + m : 8 * q + m + 1]) for m in range(8)]
            left[i] = left[i] - total(c, ql)
            right[i] = right[i] - total(c, qr)
        return rows

    def body(b, carry):
        left, right = list(carry[0]), list(carry[1])
        for q in range(nb):
            up, low = eight(left, right, q)
            r = pl.ds(pl.multiple_of(off + 8 * (b * nb + q), 8), 8)
            up = jnp.where(lane >= sub + 8 * q, up, 0.0)
            u_ref[r, off : off + HALF] = pltpu.roll(up, 8 * nb * b, 1)
            li_ref[r, off : off + HALF] = low
            left, right = left[1:] + [zero], right[1:] + [zero]
        left = [pltpu.roll(t, HALF - 8 * nb, 1) for t in left]
        return tuple(left), tuple(right)

    lax.fori_loop(0, tiles // nb, body, (left, right))


def factor(g_ref, u_ref, li_ref, service):
    h, t = slice(0, HALF), slice(HALF, PANEL)
    eliminate(g_ref[h, h], u_ref, li_ref, 0)
    service(2)
    l11 = li_ref[h, h]
    u12 = mm(l11, g_ref[h, t])
    u_ref[h, t] = u12
    u_ref[t, h] = jnp.zeros((HALF, HALF), F32)
    rest = g_ref[t, t] - mm(u12, u12, 0, 0)
    w = mm(u12, l11, 0, 0)
    li_ref[h, t] = jnp.zeros((HALF, HALF), F32)
    eliminate(rest, u_ref, li_ref, HALF)
    li_ref[t, h] = -mm(li_ref[t, t], w)
    service(2)


def kernel(scale, a_hbm, out_hbm, top_ref, bottom_ref,
           own, X, S, out, gown, ge, acc, gl, u1, li1, u2, li2, m1, m2, t1, t2,
           ec, ea, eb, lc, la, lb, ly, lx,
           load_sem, out_sem, xs, xr, ss, sr,
           e_core, e_rs, e_y, e_yr, e_ag, e_agc, l_core, l_rs, l_y, l_yr, l_x, l_ag, l_agc):
    row, y = lax.axis_index("row"), lax.axis_index("col")
    px, pz, k = row // 8, (row // 2) % 4, row % 2
    across, side = (row, 3 - y), (row, y + 1 - 2 * (y % 2))
    other = (row + 1 - 2 * k, y)

    def on_axis(h, c):
        if h == 0:
            return ((c * 4 + pz) * 2 + k, y)
        return ((px * 4 + c) * 2 + k, y)

    first = (px, pz)
    second = (pz, px)

    loads = [
        pltpu.make_async_copy(a_hbm.at[pl.ds(1024 * i, 1024)], own.at[pl.ds(1024 * i, 1024)], load_sem.at[i])
        for i in range(4)
    ]
    for c in loads:
        c.start()
    barrier = pltpu.get_barrier_semaphore()
    partners = [across, side, (row, (y + 2) % 4), other]
    for d in (1, 2, 3):
        partners += [on_axis(0, (px + d) % 4), on_axis(1, (pz + d) % 4)]
    for p in partners:
        pl.semaphore_signal(barrier, inc=1, device_id=p, device_id_type=MESH)
    pl.semaphore_wait(barrier, len(partners))
    for c in loads:
        c.wait()

    def remote(src, dst, send, recv, to):
        return pltpu.make_async_remote_copy(
            src_ref=src, dst_ref=dst, send_sem=send, recv_sem=recv, device_id=to, device_id_type=MESH
        )

    def piece(j):
        return pl.ds(pl.multiple_of(j * CHUNK, CHUNK), CHUNK)

    def to_across(j):
        return remote(own.at[piece(j)], X.at[piece(j)], xs.at[j], xr.at[j], across)

    def to_side(j, src):
        return remote(src.at[piece(j)], S.at[piece(j)], ss.at[j], sr.at[j], side)

    def each(lo, hi, f):
        def step(j, _):
            f(j)
            return 0
        lax.fori_loop(lo, hi, step, 0)

    @pl.when(y == 0)
    def _():
        def go(j):
            to_across(j).start()
            to_side((j + EARLY) % PIECES, own).start()
        each(0, PIECES, go)

    @pl.when(y == 1)
    def _():
        def go(j):
            to_across(j).start()
            to_side(j + EARLY, own).start()
        each(0, EARLY, go)
        each(EARLY, PIECES, lambda j: to_across(j).start())

    @pl.when(y >= 2)
    def _():
        each(EARLY, PIECES, lambda j: to_across(j).start())

    def forward(j):
        to_across(j).wait_recv()
        to_side(j, X).start()

    sent = [0]

    def service(n):
        lo = sent[0]
        hi = min(lo + n, PIECES)
        sent[0] = hi
        if hi > lo:
            pl.when(y >= 2)(lambda: each(lo, hi, forward))

    base = pl.multiple_of(HALF * k, HALF)
    lanes = (slice(0, HALF), slice(HALF, PANEL))

    def rows_a(h, c):
        return pl.ds(pl.multiple_of(base + 32 * c, 32), 32)

    def rows_b(h, c):
        return pl.ds(pl.multiple_of(base + 32 * first[h] + 8 * c, 8), 8)

    def scatter(ref, bc, ba, bb, sem_core, sem_rs, pause):
        n = ref.shape[0]
        c = remote(ref.at[:, pl.ds(pl.multiple_of(HALF * (1 - k), HALF), HALF)], bc, sem_core.at[0], sem_core.at[1], other)
        c.start()
        pause()
        c.wait()
        ref[:, pl.ds(base, HALF), :] += bc[...]
        cs = []
        for h in (0, 1):
            for d in (1, 2, 3):
                to = (first[h] + d) % 4
                cs.append(remote(ref.at[:, rows_a(h, to), lanes[h]], ba.at[h, d - 1],
                                 sem_rs.at[0, 0, h, d - 1], sem_rs.at[0, 1, h, d - 1], on_axis(h, to)))
        for c in cs:
            c.start()
        pause()
        for c in cs:
            c.wait()
        for h in (0, 1):
            r = rows_a(h, first[h])
            ref[:, r, lanes[h]] += (ba[h, 0] + ba[h, 1]) + ba[h, 2]
        cs = []
        for h in (0, 1):
            for d in (1, 2, 3):
                to = (second[h] + d) % 4
                cs.append(remote(ref.at[:, rows_b(h, to), lanes[h]], bb.at[h, d - 1],
                                 sem_rs.at[1, 0, h, d - 1], sem_rs.at[1, 1, h, d - 1], on_axis(1 - h, to)))
        for c in cs:
            c.start()
        pause()
        for c in cs:
            c.wait()
        for h in (0, 1):
            r = rows_b(h, second[h])
            ref[:, r, lanes[h]] += (bb[h, 0] + bb[h, 1]) + bb[h, 2]

    def gather(ref, sem_ag, sem_core, pause):
        for stage, rows, coord in ((0, rows_b, second), (1, rows_a, first)):
            cs = []
            for h in (0, 1):
                r = ref.at[:, rows(h, coord[h]), lanes[h]]
                axis = h if stage == 1 else 1 - h
                for d in (1, 2, 3):
                    cs.append(remote(r, r, sem_ag.at[stage, 0, h, d - 1], sem_ag.at[stage, 1, h, d - 1],
                                     on_axis(axis, (coord[h] + d) % 4)))
            for c in cs:
                c.start()
            pause()
            for c in cs:
                c.wait()
        r = ref.at[:, pl.ds(base, HALF)]
        c = remote(r, r, sem_core.at[0], sem_core.at[1], other)
        c.start()
        pause()
        c.wait()

    def group(g, ref):
        return ref[pl.ds(pl.multiple_of(g * GROUP, GROUP), GROUP), :]

    @pl.when(y < 2)
    def _():
        gown[...] = jnp.zeros_like(gown)
        def go(g):
            b = group(g, own)
            gown[0] += mm(b, b, 0, 0)
        each(0, ROWS // GROUP, go)
        scatter(gown, ec, ea, eb, e_core, e_rs, lambda: None)
        for h in (0, 1):
            r = rows_b(h, second[h])
            ge[y, r, lanes[h]] = gown[0, r, lanes[h]]

    acc[...] = jnp.zeros_like(acc)

    def inner(g):
        o, x, s = group(g, own), group(g, X), group(g, S)

        @pl.when(y == 0)
        def _():
            acc[1] += mm(o, x, 0, 0)
            acc[2] += mm(s, x, 0, 0)

        @pl.when(y == 1)
        def _():
            acc[0] += mm(s, o, 0, 0)
            acc[1] += mm(s, x, 0, 0)
            acc[2] += mm(o, x, 0, 0)

        @pl.when(y == 2)
        def _():
            acc[1] += mm(s, o, 0, 0)
            acc[2] += mm(x, o, 0, 0)

        @pl.when(y == 3)
        def _():
            acc[0] += mm(x, s, 0, 0)
            acc[1] += mm(x, o, 0, 0)
            acc[2] += mm(s, o, 0, 0)

    def arrived(g):
        each(4 * g, 4 * g + 4, lambda j: to_side(j, X).wait_recv())

    service(5)
    pl.when(y >= 2)(lambda: arrived(0))
    pl.when(y >= 2)(lambda: inner(0))
    service(2)

    def to_y(src_y, ref, h, d, send, recv):
        return remote(ref, ref, send, recv, (row, (y + d) % 4))

    shard = [(h, rows_b(h, second[h])) for h in (0, 1)]

    @pl.when(y < 2)
    def _():
        cs = []
        for h, r in shard:
            v = ge.at[y, r, lanes[h]]
            for d in (1, 2, 3):
                cs.append(remote(v, v, e_y.at[h, d - 1], e_yr.at[y, h], (row, (y + d) % 4)))
        for c in cs:
            c.start()
        for c in cs:
            c.wait_send()

    for src in (0, 1):
        @pl.when(y != src)
        def _():
            for h, r in shard:
                v = ge.at[src, r, lanes[h]]
                remote(v, v, e_y.at[h, 0], e_yr.at[src, h], (row, src)).wait_recv()

    gather(ge, e_ag, e_agc, lambda: service(1))
    pl.when(y >= 2)(lambda: arrived(1))
    pl.when(y >= 2)(lambda: inner(1))
    ge[...] = ge[...] * scale
    factor(ge.at[0], u1, li1, service)

    service(EARLY - sent[0])

    @pl.when(y < 2)
    def _():
        def go(g):
            def got(j):
                to_across(j).wait_recv()
                to_side(j, own).wait_recv()
            each(4 * g, 4 * g + 4, got)
            inner(g)
        each(4, 8, go)

    @pl.when(y >= 2)
    def _():
        def go(g):
            arrived(g)
            inner(g)
        each(2, 4, go)

    scatter(acc, lc, la, lb, l_core, l_rs, lambda: service(1))
    cs = []
    for h, r in shard:
        cs.append(remote(acc.at[pl.ds(1, 2), r, lanes[h]], lx.at[h], l_x.at[0, h], l_x.at[1, h], across))
    for c in cs:
        c.start()
    for h, r in shard:
        t1[r, lanes[h]] = acc[0, r, lanes[h]]

    @pl.when(y % 2 == 1)
    def _():
        es = []
        for h, r in shard:
            v = t1.at[r, lanes[h]]
            for d in (1, 2, 3):
                es.append(remote(v, ly.at[y // 2, h], l_y.at[h, d - 1], l_yr.at[y // 2, h], (row, (y + d) % 4)))
        for c in es:
            c.start()
        for c in es:
            c.wait_send()
        for h, r in shard:
            ly[y // 2, h] = t1[r, lanes[h]]

    service(1)
    for src in (1, 3):
        @pl.when(y != src)
        def _():
            for h, r in shard:
                remote(t1.at[r, lanes[h]], ly.at[src // 2, h], l_y.at[h, 0], l_yr.at[src // 2, h], (row, src)).wait_recv()
    for c in cs:
        c.wait()
    for h, r in shard:
        gl[0, r, lanes[h]] = ly[0, h] + ly[1, h]
        gl[1:3, r, lanes[h]] = acc[1:3, r, lanes[h]] + lx[h]
    gather(gl, l_ag, l_agc, lambda: service(1))

    c01 = mm(li1[...], gl[0] * scale)
    t1[...] = c01
    t2[...] = ge[1] - mm(c01, c01, 0, 0)
    service(1)
    factor(t2, u2, li2, service)
    c0j = mm(li1[...], gl[1] * scale)
    c01 = t1[...]
    coeff2 = mm(li2[...], gl[2] * scale - mm(c01, c0j, 0, 0))
    zero = jnp.zeros((PANEL, PANEL), F32)

    @pl.when(y == 0)
    def _():
        top_ref[...] = u1[...]
        bottom_ref[...] = zero
        m1[...] = li1[...].T

    @pl.when(y == 1)
    def _():
        top_ref[...] = t1[...]
        bottom_ref[...] = u2[...]
        m1[...] = li2[...].T
        m2[...] = mm(mm(li1[...], t1[...], 0, 0), li2[...], 1, 1)

    @pl.when(y >= 2)
    def _():
        top_ref[...] = c0j
        bottom_ref[...] = coeff2
        zz = mm(li2[...], coeff2, 0, 0)
        yy = mm(li1[...], c0j - mm(c01, zz), 0, 0)

        @pl.when(y == 2)
        def _():
            m1[...] = zz
            m2[...] = yy

        @pl.when(y == 3)
        def _():
            m1[...] = yy
            m2[...] = zz

    per = APPLY // CHUNK
    steps = ROWS // APPLY

    def part(g):
        return pl.ds(pl.multiple_of(g * APPLY, APPLY), APPLY)

    def store(g):
        return pltpu.make_async_copy(out.at[part(g)], out_hbm.at[part(g)], out_sem.at[g])

    @pl.when(y == 0)
    def _():
        def go(g):
            out[part(g), :] = mm(own[part(g), :], m1[...])
            store(g).start()
        each(0, steps, go)

    @pl.when(y == 1)
    def _():
        def go(i):
            g = (i + steps // 2) % steps
            pl.when(g < steps // 2)(lambda: each(per * g, per * g + per, lambda j: to_side(j, own).wait_recv()))
            out[part(g), :] = mm(own[part(g), :], m1[...]) - mm(S[part(g), :], m2[...])
            store(g).start()
        each(0, steps, go)

    done = sent[0]

    @pl.when(y >= 2)
    def _():
        def reach(g):
            return jnp.minimum(jnp.maximum(done + g // 3, per * g + per), PIECES)
        def go(g):
            each(jnp.where(g == 0, done, reach(g - 1)), reach(g), forward)
            pl.when(g >= steps // 2)(lambda: each(per * g, per * g + per, lambda j: to_side(j, X).wait_recv()))
            out[part(g), :] = (own[part(g), :] - mm(X[part(g), :], m1[...])) - mm(S[part(g), :], m2[...])
            store(g).start()
        each(0, steps, go)

    @pl.when(y < 2)
    def _():
        each(0, EARLY, lambda j: to_across(j).wait_send())

    @pl.when(y != 1)
    def _():
        each(0, EARLY, lambda j: to_side(j, own).wait_send())

    def late(j):
        to_across(j).wait_send()
        to_side(j, own).wait_send()
    each(EARLY, PIECES, late)
    each(0, steps, lambda g: store(g).wait())


def on_device(total_rows, influence):
    vmem = lambda *s: pltpu.VMEM(s, F32)
    dma = lambda *s: pltpu.SemaphoreType.DMA(s)
    square = jax.ShapeDtypeStruct((PANEL, PANEL), F32)
    block = vmem(PANEL, PANEL)
    factored, top, bottom = pl.pallas_call(
        functools.partial(kernel, 1.0 / total_rows),
        name="factor_panels",
        out_shape=[jax.ShapeDtypeStruct((ROWS, PANEL), F32), square, square],
        in_specs=[pl.BlockSpec(memory_space=pl.ANY)],
        out_specs=[pl.BlockSpec(memory_space=pl.ANY)] + [pl.BlockSpec(memory_space=pltpu.VMEM)] * 2,
        scratch_shapes=[
            vmem(ROWS, PANEL), vmem(ROWS, PANEL), vmem(ROWS, PANEL), vmem(ROWS, PANEL),
            vmem(1, PANEL, PANEL), vmem(2, PANEL, PANEL), vmem(3, PANEL, PANEL), vmem(3, PANEL, PANEL),
            block, block, block, block, block, block, block, block,
            vmem(1, HALF, PANEL), vmem(2, 3, 1, 32, HALF), vmem(2, 3, 1, 8, HALF),
            vmem(3, HALF, PANEL), vmem(2, 3, 3, 32, HALF), vmem(2, 3, 3, 8, HALF),
            vmem(2, 2, 8, HALF), vmem(2, 2, 8, HALF),
            dma(4), dma(ROWS // APPLY), dma(PIECES), dma(PIECES), dma(PIECES), dma(PIECES),
            dma(2), dma(2, 2, 2, 3), dma(2, 3), dma(2, 2), dma(2, 2, 2, 3), dma(2),
            dma(2), dma(2, 2, 2, 3), dma(2, 3), dma(2, 2), dma(2, 2), dma(2, 2, 2, 3), dma(2),
        ],
        compiler_params=pltpu.CompilerParams(
            collective_id=0, has_side_effects=True, vmem_limit_bytes=56 * 2**20
        ),
    )(influence)
    return factored, jnp.concatenate([top, bottom], axis=0)


def solution(mesh):
    total_rows = ROWS * mesh.shape["row"]
    return jax.shard_map(
        functools.partial(on_device, total_rows),
        mesh=mesh,
        in_specs=(P("row", "col"),),
        out_specs=(P("row", "col"), P(None, "col")),
        check_vma=False,
    )
```

```python
import functools

import jax
import jax.numpy as jnp
from jax import lax
from jax.experimental import pallas as pl
from jax.experimental.pallas import tpu as pltpu
from jax.sharding import PartitionSpec as P

MESH = pl.DeviceIdType.MESH
F32 = jnp.float32
PANEL = 256
HALF = 128
ROWS = 4096
CHUNK = 128
PIECES = ROWS // CHUNK
EARLY = PIECES // 2
GROUP = 256
LAG = 3
APPLY = 256


def mm(a, b, ca=1, cb=0):
    return lax.dot_general(
        a, b, (((ca,), (cb,)), ((), ())),
        precision=lax.Precision.HIGHEST, preferred_element_type=F32,
    )


def spread(v):
    return jnp.broadcast_to(v, (8, HALF))


def eliminate(square, u_ref, li_ref, hook, nb=4):
    sub = lax.broadcasted_iota(jnp.int32, (8, HALF), 0)
    lane = lax.broadcasted_iota(jnp.int32, (8, HALF), 1)
    zero = jnp.zeros((8, HALF), F32)
    tiles = HALF // 8
    left = tuple(square[8 * i : 8 * i + 8, :] for i in range(tiles))
    right = tuple(jnp.where(lane == sub + 8 * i, 1.0, 0.0).astype(F32) for i in range(tiles))

    def eight(left, right, q):
        w = [spread(left[0][:, 8 * q + m : 8 * q + m + 1]) for m in range(8)] + [left[0], right[0]]
        rows = [zero, zero]
        for j in range(0, 8, 2):
            pivot = (sub == j) | (sub == j + 1)
            p00, p01, p11 = spread(w[j][j : j + 1]), spread(w[j][j + 1 : j + 2]), spread(w[j + 1][j + 1 : j + 2])
            rd = 1.0 / (p00 * p11 - p01 * p01)
            i00, i01, i11 = p11 * rd, p01 * rd, p00 * rd
            u, v = jnp.where(pivot, 0.0, w[j]), jnp.where(pivot, 0.0, w[j + 1])
            s0 = lax.rsqrt(p00)
            m0 = p01 * (s0 * s0)
            s1 = lax.rsqrt(p11 - m0 * p01)
            for t in list(range(j + 2, 8)) + [8, 9]:
                r0, r1 = spread(w[t][j : j + 1]), spread(w[t][j + 1 : j + 2])
                a, b = r0 * i00 - r1 * i01, r1 * i11 - r0 * i01
                if t >= 8:
                    rows[t - 8] = jnp.where(
                        sub == j, r0 * s0, jnp.where(sub == j + 1, (r1 - m0 * r0) * s1, rows[t - 8])
                    )
                w[t] = jnp.where(sub == j, a, jnp.where(sub == j + 1, b, w[t] - (u * a + v * b)))
        ql = [spread(w[8][m : m + 1]) for m in range(8)]
        qr = [spread(w[9][m : m + 1]) for m in range(8)]

        def total(c, q):
            t = [c[m] * q[m] for m in range(8)]
            return ((t[0] + t[1]) + (t[2] + t[3])) + ((t[4] + t[5]) + (t[6] + t[7]))

        for i in range(1, tiles):
            c = [spread(left[i][:, 8 * q + m : 8 * q + m + 1]) for m in range(8)]
            left[i] = left[i] - total(c, ql)
            right[i] = right[i] - total(c, qr)
        return rows

    def body(b, carry):
        left, right = list(carry[0]), list(carry[1])
        for q in range(nb):
            up, low = eight(left, right, q)
            r = pl.ds(pl.multiple_of(8 * (b * nb + q), 8), 8)
            up = jnp.where(lane >= sub + 8 * q, up, 0.0)
            u_ref[r, :] = pltpu.roll(up, 8 * nb * b, 1)
            li_ref[r, :] = low
            left, right = left[1:] + [zero], right[1:] + [zero]
        left = [pltpu.roll(t, HALF - 8 * nb, 1) for t in left]
        hook(b)
        return tuple(left), tuple(right)

    lax.fori_loop(0, tiles // nb, body, (left, right))


HEAD, TAIL = slice(0, HALF), slice(HALF, PANEL)


def factor(g_ref, u_ref, li_ref, parts, us, ls, hook):
    parts[0] = g_ref[HEAD, HEAD]

    def block(p, _):
        eliminate(parts[p], us.at[p], ls.at[p], functools.partial(hook, p))

        @pl.when(p == 0)
        def _():
            l11 = ls[0]
            u12 = mm(l11, g_ref[HEAD, TAIL])
            u_ref[HEAD, TAIL] = u12
            parts[1] = g_ref[TAIL, TAIL] - mm(u12, u12, 0, 0)
            li_ref[TAIL, HEAD] = mm(u12, l11, 0, 0)
        return 0

    lax.fori_loop(0, 2, block, 0)
    li_ref[TAIL, HEAD] = -mm(ls[1], li_ref[TAIL, HEAD])
    for p, c in ((0, HEAD), (1, TAIL)):
        u_ref[c, c] = us[p]
        li_ref[c, c] = ls[p]
    u_ref[TAIL, HEAD] = jnp.zeros((HALF, HALF), F32)
    li_ref[HEAD, TAIL] = jnp.zeros((HALF, HALF), F32)


def kernel(scale, a_hbm, out_hbm, upper_ref,
           own, X, S, out, gown, ge, acc, gl, u1, li1, u2, li2, m1, m2, t1, t2, parts, us, ls,
           ec, ea, eb, lc, la, lb, ly, lx,
           load_sem, out_sem, xs, xr, ss, sr,
           e_core, e_rs, e_y, e_yr, e_ag, e_agc, l_core, l_rs, l_y, l_yr, l_x, l_ag, l_agc):
    row, y = lax.axis_index("row"), lax.axis_index("col")
    px, pz, k = row // 8, (row // 2) % 4, row % 2
    across, side = (row, 3 - y), (row, y + 1 - 2 * (y % 2))
    other = (row + 1 - 2 * k, y)

    def on_axis(h, c):
        if h == 0:
            return ((c * 4 + pz) * 2 + k, y)
        return ((px * 4 + c) * 2 + k, y)

    first = (px, pz)
    second = (pz, px)

    loads = [
        pltpu.make_async_copy(a_hbm.at[pl.ds(1024 * i, 1024)], own.at[pl.ds(1024 * i, 1024)], load_sem.at[i])
        for i in range(4)
    ]
    for c in loads:
        c.start()
    barrier = pltpu.get_barrier_semaphore()
    partners = [across, side, (row, (y + 2) % 4), other]
    for d in (1, 2, 3):
        partners += [on_axis(0, (px + d) % 4), on_axis(1, (pz + d) % 4)]
    for p in partners:
        pl.semaphore_signal(barrier, inc=1, device_id=p, device_id_type=MESH)
    pl.semaphore_wait(barrier, len(partners))
    for c in loads:
        c.wait()

    def remote(src, dst, send, recv, to):
        return pltpu.make_async_remote_copy(
            src_ref=src, dst_ref=dst, send_sem=send, recv_sem=recv, device_id=to, device_id_type=MESH
        )

    def piece(j):
        return pl.ds(pl.multiple_of(j * CHUNK, CHUNK), CHUNK)

    def to_across(j):
        return remote(own.at[piece(j)], X.at[piece(j)], xs.at[j], xr.at[j], across)

    def to_side(j, src):
        return remote(src.at[piece(j)], S.at[piece(j)], ss.at[j], sr.at[j], side)

    def each(lo, hi, f):
        def step(j, _):
            f(j)
            return 0
        lax.fori_loop(lo, hi, step, 0)

    ahead = 3

    @pl.when(y >= 2)
    def _():
        each(EARLY, EARLY + ahead, lambda j: to_across(j).start())

    def forward(j):
        to_across(j).wait_recv()
        to_side(j, X).start()

        @pl.when(j < EARLY - ahead)
        def _():
            to_across(EARLY + j).wait_send()
            to_across(EARLY + ahead + j).start()

    def turned(j):
        return (j + EARLY) % PIECES

    def sided(j):
        return (y == 0) | (j < EARLY)

    def old_piece(j):
        to_across(j).wait_send()
        pl.when(sided(j))(lambda: to_side(turned(j), own).wait_send())

    def new_piece(j):
        pl.when(j >= LAG)(lambda: old_piece(j - LAG))
        to_across(j).start()
        pl.when(sided(j))(lambda: to_side(turned(j), own).start())

    sent, passed = [0], [0]

    def source(n):
        lo, hi = sent[0], min(sent[0] + n, PIECES)
        sent[0] = hi
        if hi > lo:
            pl.when(y < 2)(lambda: each(lo, hi, new_piece))

    def sink(n):
        lo, hi = passed[0], min(passed[0] + n, PIECES)
        passed[0] = hi
        if hi > lo:
            pl.when(y >= 2)(lambda: each(lo, hi, forward))

    def service(n):
        source(n)
        sink(n)

    def hooked(lo, past):
        def hook(p, b):
            j = 2 * p + b // 2
            pl.when((b % 2 == 1) & (y < 2) & (lo + j < PIECES))(lambda: new_piece(lo + j))
            pl.when((b % 2 == 1) & (y >= 2) & (past + j < PIECES))(lambda: forward(past + j))
        return hook

    base = pl.multiple_of(HALF * k, HALF)
    lanes = (slice(0, HALF), slice(HALF, PANEL))

    def rows_a(h, c):
        return pl.ds(pl.multiple_of(base + 32 * c, 32), 32)

    def rows_b(h, c):
        return pl.ds(pl.multiple_of(base + 32 * first[h] + 8 * c, 8), 8)

    def scatter(ref, bc, ba, bb, sem_core, sem_rs, pauses):
        n = ref.shape[0]
        c = remote(ref.at[:, pl.ds(pl.multiple_of(HALF * (1 - k), HALF), HALF)], bc, sem_core.at[0], sem_core.at[1], other)
        c.start()
        pauses[0]()
        c.wait()
        ref[:, pl.ds(base, HALF), :] += bc[...]
        cs = []
        for h in (0, 1):
            for d in (1, 2, 3):
                to = (first[h] + d) % 4
                cs.append(remote(ref.at[:, rows_a(h, to), lanes[h]], ba.at[h, d - 1],
                                 sem_rs.at[0, 0, h, d - 1], sem_rs.at[0, 1, h, d - 1], on_axis(h, to)))
        for c in cs:
            c.start()
        pauses[1]()
        for c in cs:
            c.wait()
        for h in (0, 1):
            r = rows_a(h, first[h])
            ref[:, r, lanes[h]] += (ba[h, 0] + ba[h, 1]) + ba[h, 2]
        cs = []
        for h in (0, 1):
            for d in (1, 2, 3):
                to = (second[h] + d) % 4
                cs.append(remote(ref.at[:, rows_b(h, to), lanes[h]], bb.at[h, d - 1],
                                 sem_rs.at[1, 0, h, d - 1], sem_rs.at[1, 1, h, d - 1], on_axis(1 - h, to)))
        for c in cs:
            c.start()
        pauses[2]()
        for c in cs:
            c.wait()
        for h in (0, 1):
            r = rows_b(h, second[h])
            ref[:, r, lanes[h]] += (bb[h, 0] + bb[h, 1]) + bb[h, 2]

    def gather_axis(ref, sem_ag, stage, pause):
        rows, coord = ((rows_b, second), (rows_a, first))[stage]
        cs = []
        for h in (0, 1):
            r = ref.at[:, rows(h, coord[h]), lanes[h]]
            axis = h if stage == 1 else 1 - h
            for d in (1, 2, 3):
                cs.append(remote(r, r, sem_ag.at[stage, 0, h, d - 1], sem_ag.at[stage, 1, h, d - 1],
                                 on_axis(axis, (coord[h] + d) % 4)))
        for c in cs:
            c.start()
        pause()
        for c in cs:
            c.wait()

    def gather_core(ref, sem_core, pause):
        r = ref.at[:, pl.ds(base, HALF)]
        c = remote(r, r, sem_core.at[0], sem_core.at[1], other)
        c.start()
        pause()
        c.wait()

    def group(g, ref):
        return ref[pl.ds(pl.multiple_of(g * GROUP, GROUP), GROUP), :]

    source(3)

    @pl.when(y < 2)
    def _():
        gown[...] = jnp.zeros_like(gown)

        def go(g):
            b = group(g, own)
            gown[0] += mm(b, b, 0, 0)
            pl.when(g % 8 == 7)(lambda: new_piece(3 + g // 8))
        each(0, ROWS // GROUP, go)
        sent[0] = 5
        scatter(gown, ec, ea, eb, e_core, e_rs, [lambda: source(1)] * 3)
        for h in (0, 1):
            r = rows_b(h, second[h])
            ge[y, r, lanes[h]] = gown[0, r, lanes[h]]

    acc[...] = jnp.zeros_like(acc)

    def inner(g):
        def two(a, b, c):
            both = mm(jnp.concatenate([group(g, a), group(g, b)], axis=1), group(g, c), 0, 0)
            acc[1] += both[:PANEL]
            acc[2] += both[PANEL:]

        def one(a, b):
            acc[0] += mm(group(g, a), group(g, b), 0, 0)

        @pl.when(y == 0)
        def _():
            two(own, S, X)

        @pl.when(y == 1)
        def _():
            two(S, own, X)
            one(S, own)

        @pl.when(y == 2)
        def _():
            two(S, X, own)

        @pl.when(y == 3)
        def _():
            two(X, S, own)
            one(X, S)

    shard = [(h, rows_b(h, second[h])) for h in (0, 1)]

    def shard_sends():
        return [
            remote(v, v, e_y.at[h, d - 1], e_yr.at[y, h], (row, (y + d) % 4))
            for h, r in shard for v in [ge.at[y, r, lanes[h]]] for d in (1, 2, 3)
        ]

    @pl.when(y < 2)
    def _():
        for c in shard_sends():
            c.start()

    source(1)
    sink(2)
    QUARTER = EARLY // 4

    def step(i, _):
        @pl.when(y < 2)
        def _():
            new_piece(jnp.where(i == 3, 18, 9 + 2 * i))
            def got(j):
                to_across(j).wait_recv()
                to_side(j, own).wait_recv()
            each(EARLY + QUARTER * i, EARLY + QUARTER * i + QUARTER, got)
            each(8 + 2 * i, 10 + 2 * i, inner)
            pl.when(i < 2)(lambda: new_piece(10 + 2 * i))

        @pl.when(y >= 2)
        def _():
            pl.when(i < 3)(lambda: each(4 * i + 2, 4 * i + 4, forward))
            each(QUARTER * i, QUARTER * i + QUARTER, lambda j: to_side(j, X).wait_recv())
            each(2 * i, 2 * i + 2, inner)
            pl.when(i < 2)(lambda: each(4 * i + 4, 4 * i + 6, forward))
            pl.when(i == 2)(lambda: forward(12))

        @pl.when(i == 0)
        def _():
            @pl.when(y < 2)
            def _():
                for c in shard_sends():
                    c.wait_send()
            for src in (0, 1):
                @pl.when(y != src)
                def _():
                    for h, r in shard:
                        v = ge.at[src, r, lanes[h]]
                        remote(v, v, e_y.at[h, 0], e_yr.at[src, h], (row, src)).wait_recv()
            gather_axis(ge, e_ag, 0, lambda: None)

        @pl.when(i == 1)
        def _():
            gather_axis(ge, e_ag, 1, lambda: None)
            gather_core(ge, e_agc, lambda: None)

        @pl.when(i == 2)
        def _():
            ge[...] = ge[...] * scale
            factor(ge.at[0], u1, li1, parts, us, ls, hooked(14, 13))
        return 0

    lax.fori_loop(0, 4, step, 0)
    sent[0], passed[0] = 19, 17

    scatter(acc, lc, la, lb, l_core, l_rs, [lambda: service(1), lambda: service(2), lambda: service(1)])
    cs = []
    for h, r in shard:
        cs.append(remote(acc.at[pl.ds(1, 2), r, lanes[h]], lx.at[h], l_x.at[0, h], l_x.at[1, h], across))
    for c in cs:
        c.start()
    for h, r in shard:
        t1[r, lanes[h]] = acc[0, r, lanes[h]]

    @pl.when(y % 2 == 1)
    def _():
        es = []
        for h, r in shard:
            v = t1.at[r, lanes[h]]
            for d in (1, 2, 3):
                es.append(remote(v, ly.at[y // 2, h], l_y.at[h, d - 1], l_yr.at[y // 2, h], (row, (y + d) % 4)))
        for c in es:
            c.start()
        for c in es:
            c.wait_send()
        for h, r in shard:
            ly[y // 2, h] = t1[r, lanes[h]]

    service(2)
    for src in (1, 3):
        @pl.when(y != src)
        def _():
            for h, r in shard:
                remote(t1.at[r, lanes[h]], ly.at[src // 2, h], l_y.at[h, 0], l_yr.at[src // 2, h], (row, src)).wait_recv()
    for c in cs:
        c.wait()
    for h, r in shard:
        gl[0, r, lanes[h]] = ly[0, h] + ly[1, h]
        gl[1:3, r, lanes[h]] = acc[1:3, r, lanes[h]] + lx[h]
    gather_axis(gl, l_ag, 0, lambda: service(1))
    gather_axis(gl, l_ag, 1, lambda: service(2))
    gather_core(gl, l_agc, lambda: service(1))

    c01 = mm(li1[...], gl[0] * scale)
    t1[...] = c01
    t2[...] = ge[1] - mm(c01, c01, 0, 0)
    factor(t2, u2, li2, parts, us, ls, hooked(sent[0], passed[0]))
    sent[0], passed[0] = min(sent[0] + 4, PIECES), min(passed[0] + 4, PIECES)
    source(PIECES)
    c0j = mm(li1[...], gl[1] * scale)
    c01 = t1[...]
    coeff2 = mm(li2[...], gl[2] * scale - mm(c01, c0j, 0, 0))
    zero = jnp.zeros((PANEL, PANEL), F32)

    @pl.when(y == 0)
    def _():
        upper_ref[:PANEL] = u1[...]
        upper_ref[PANEL:] = zero
        m1[...] = li1[...].T

    @pl.when(y == 1)
    def _():
        upper_ref[:PANEL] = t1[...]
        upper_ref[PANEL:] = u2[...]
        m1[...] = li2[...].T
        m2[...] = mm(mm(li1[...], t1[...], 0, 0), li2[...], 1, 1)

    @pl.when(y >= 2)
    def _():
        upper_ref[:PANEL] = c0j
        upper_ref[PANEL:] = coeff2
        zz = mm(li2[...], coeff2, 0, 0)
        yy = mm(li1[...], c0j - mm(c01, zz), 0, 0)

        @pl.when(y == 2)
        def _():
            m1[...] = zz
            m2[...] = yy

        @pl.when(y == 3)
        def _():
            m1[...] = yy
            m2[...] = zz

    per = APPLY // CHUNK
    steps = ROWS // APPLY

    def part(g):
        return pl.ds(pl.multiple_of(g * APPLY, APPLY), APPLY)

    def store(g):
        return pltpu.make_async_copy(out.at[part(g)], out_hbm.at[part(g)], out_sem.at[g])

    @pl.when(y == 0)
    def _():
        def go(g):
            out[part(g), :] = mm(own[part(g), :], m1[...])
            store(g).start()
        each(0, steps, go)

    @pl.when(y == 1)
    def _():
        def go(i):
            g = (i + steps // 2) % steps
            pl.when(g < steps // 2)(lambda: each(per * g, per * g + per, lambda j: to_side(j, own).wait_recv()))
            out[part(g), :] = mm(own[part(g), :], m1[...]) - mm(S[part(g), :], m2[...])
            store(g).start()
        each(0, steps, go)

    done = passed[0]

    @pl.when(y >= 2)
    def _():
        def reach(g):
            return jnp.minimum(jnp.maximum(done + g // 3, per * g + per), PIECES)
        def go(g):
            each(jnp.where(g == 0, done, reach(g - 1)), reach(g), forward)
            pl.when(g >= steps // 2)(lambda: each(per * g, per * g + per, lambda j: to_side(j, X).wait_recv()))
            out[part(g), :] = (own[part(g), :] - mm(X[part(g), :], m1[...])) - mm(S[part(g), :], m2[...])
            store(g).start()
        each(0, steps, go)

    @pl.when(y < 2)
    def _():
        each(PIECES - LAG, PIECES, old_piece)

    @pl.when(y >= 2)
    def _():
        each(PIECES - ahead, PIECES, lambda j: to_across(j).wait_send())
        each(0, PIECES, lambda j: to_side(j, X).wait_send())

    each(0, steps, lambda g: store(g).wait())


def on_device(total_rows, influence):
    vmem = lambda *s: pltpu.VMEM(s, F32)
    dma = lambda *s: pltpu.SemaphoreType.DMA(s)
    block = vmem(PANEL, PANEL)
    factored, upper = pl.pallas_call(
        functools.partial(kernel, 1.0 / total_rows),
        name="factor_panels",
        out_shape=[jax.ShapeDtypeStruct((ROWS, PANEL), F32), jax.ShapeDtypeStruct((2 * PANEL, PANEL), F32)],
        in_specs=[pl.BlockSpec(memory_space=pl.ANY)],
        out_specs=[pl.BlockSpec(memory_space=pl.ANY)] + [pl.BlockSpec(memory_space=pltpu.VMEM)],
        scratch_shapes=[
            vmem(ROWS, PANEL), vmem(ROWS, PANEL), vmem(ROWS, PANEL), vmem(ROWS, PANEL),
            vmem(1, PANEL, PANEL), vmem(2, PANEL, PANEL), vmem(3, PANEL, PANEL), vmem(3, PANEL, PANEL),
            block, block, block, block, block, block, block, block,
            vmem(2, HALF, HALF), vmem(2, HALF, HALF), vmem(2, HALF, HALF),
            vmem(1, HALF, PANEL), vmem(2, 3, 1, 32, HALF), vmem(2, 3, 1, 8, HALF),
            vmem(3, HALF, PANEL), vmem(2, 3, 3, 32, HALF), vmem(2, 3, 3, 8, HALF),
            vmem(2, 2, 8, HALF), vmem(2, 2, 8, HALF),
            dma(4), dma(ROWS // APPLY), dma(PIECES), dma(PIECES), dma(PIECES), dma(PIECES),
            dma(2), dma(2, 2, 2, 3), dma(2, 3), dma(2, 2), dma(2, 2, 2, 3), dma(2),
            dma(2), dma(2, 2, 2, 3), dma(2, 3), dma(2, 2), dma(2, 2), dma(2, 2, 2, 3), dma(2),
        ],
        compiler_params=pltpu.CompilerParams(
            collective_id=0, has_side_effects=True, vmem_limit_bytes=56 * 2**20
        ),
    )(influence)
    return factored, upper


def solution(mesh):
    total_rows = ROWS * mesh.shape["row"]
    return jax.shard_map(
        functools.partial(on_device, total_rows),
        mesh=mesh,
        in_specs=(P("row", "col"),),
        out_specs=(P("row", "col"), P(None, "col")),
        check_vma=False,
    )
```

```python
import functools

import jax
import jax.numpy as jnp
from jax import lax
from jax.experimental import pallas as pl
from jax.experimental.pallas import tpu as pltpu
from jax.sharding import PartitionSpec as P

MESH = pl.DeviceIdType.MESH
F32 = jnp.float32
PANEL = 256
HALF = 128
ROWS = 4096
CHUNK = 128
PIECES = ROWS // CHUNK
EARLY = PIECES // 2
GROUP = 256
EXTRA = 1
LAG = 6
APPLY = 512


def mm(a, b, ca=1, cb=0):
    return lax.dot_general(
        a, b, (((ca,), (cb,)), ((), ())),
        precision=lax.Precision.HIGHEST, preferred_element_type=F32,
    )


BF16 = jnp.bfloat16
TERMS = ((2, 0), (0, 2), (1, 1), (1, 0), (0, 1), (0, 0))


def three(a):
    high = a.astype(BF16)
    rest = a - high.astype(F32)
    middle = rest.astype(BF16)
    return high, middle, (rest - middle.astype(F32)).astype(BF16)


def stacked(parts_of, side, axis):
    return jnp.concatenate([p[t[side]] for t in TERMS for p in parts_of], axis=axis)


def spread(v):
    return jnp.broadcast_to(v, (8, HALF))


def eliminate(square, u_ref, li_ref, hook, nb=4):
    sub = lax.broadcasted_iota(jnp.int32, (8, HALF), 0)
    lane = lax.broadcasted_iota(jnp.int32, (8, HALF), 1)
    zero = jnp.zeros((8, HALF), F32)
    tiles = HALF // 8
    left = tuple(square[8 * i : 8 * i + 8, :] for i in range(tiles))
    right = tuple(jnp.where(lane == sub + 8 * i, 1.0, 0.0).astype(F32) for i in range(tiles))

    def eight(left, right, q):
        w = [spread(left[0][:, 8 * q + m : 8 * q + m + 1]) for m in range(8)] + [left[0], right[0]]
        rows = [zero, zero]
        for j in range(0, 8, 2):
            pivot = (sub == j) | (sub == j + 1)
            p00, p01, p11 = spread(w[j][j : j + 1]), spread(w[j][j + 1 : j + 2]), spread(w[j + 1][j + 1 : j + 2])
            rd = 1.0 / (p00 * p11 - p01 * p01)
            i00, i01, i11 = p11 * rd, p01 * rd, p00 * rd
            u, v = jnp.where(pivot, 0.0, w[j]), jnp.where(pivot, 0.0, w[j + 1])
            s0 = lax.rsqrt(p00)
            m0 = p01 * (s0 * s0)
            s1 = lax.rsqrt(p11 - m0 * p01)
            for t in list(range(j + 2, 8)) + [8, 9]:
                r0, r1 = spread(w[t][j : j + 1]), spread(w[t][j + 1 : j + 2])
                a, b = r0 * i00 - r1 * i01, r1 * i11 - r0 * i01
                if t >= 8:
                    rows[t - 8] = jnp.where(
                        sub == j, r0 * s0, jnp.where(sub == j + 1, (r1 - m0 * r0) * s1, rows[t - 8])
                    )
                w[t] = jnp.where(sub == j, a, jnp.where(sub == j + 1, b, w[t] - (u * a + v * b)))
        ql = [spread(w[8][m : m + 1]) for m in range(8)]
        qr = [spread(w[9][m : m + 1]) for m in range(8)]

        def total(c, q):
            t = [c[m] * q[m] for m in range(8)]
            return ((t[0] + t[1]) + (t[2] + t[3])) + ((t[4] + t[5]) + (t[6] + t[7]))

        for i in range(1, tiles):
            c = [spread(left[i][:, 8 * q + m : 8 * q + m + 1]) for m in range(8)]
            left[i] = left[i] - total(c, ql)
            right[i] = right[i] - total(c, qr)
        return rows

    def body(b, carry):
        left, right = list(carry[0]), list(carry[1])
        for q in range(nb):
            up, low = eight(left, right, q)
            r = pl.ds(pl.multiple_of(8 * (b * nb + q), 8), 8)
            up = jnp.where(lane >= sub + 8 * q, up, 0.0)
            u_ref[r, :] = pltpu.roll(up, 8 * nb * b, 1)
            li_ref[r, :] = low
            left, right = left[1:] + [zero], right[1:] + [zero]
        left = [pltpu.roll(t, HALF - 8 * nb, 1) for t in left]
        hook(b)
        return tuple(left), tuple(right)

    lax.fori_loop(0, tiles // nb, body, (left, right))


HEAD, TAIL = slice(0, HALF), slice(HALF, PANEL)


def factor(g_ref, u_ref, li_ref, parts, us, ls, hook):
    parts[0] = g_ref[HEAD, HEAD]

    def block(p, _):
        eliminate(parts[p], us.at[p], ls.at[p], functools.partial(hook, p))

        @pl.when(p == 0)
        def _():
            l11 = ls[0]
            u12 = mm(l11, g_ref[HEAD, TAIL])
            u_ref[HEAD, TAIL] = u12
            parts[1] = g_ref[TAIL, TAIL] - mm(u12, u12, 0, 0)
            li_ref[TAIL, HEAD] = mm(u12, l11, 0, 0)
        return 0

    lax.fori_loop(0, 2, block, 0)
    li_ref[TAIL, HEAD] = -mm(ls[1], li_ref[TAIL, HEAD])
    for p, c in ((0, HEAD), (1, TAIL)):
        u_ref[c, c] = us[p]
        li_ref[c, c] = ls[p]
    u_ref[TAIL, HEAD] = jnp.zeros((HALF, HALF), F32)
    li_ref[HEAD, TAIL] = jnp.zeros((HALF, HALF), F32)


def kernel(scale, a_hbm, out_hbm, upper_ref,
           own, X, S, out, gown, ge, acc, gl, u1, u2, m1, m2, mcat, sq, parts, us, ls,
           ec, ea, eb, lc, la, lb, ly, lx,
           load_sem, out_sem, xs, xr, ss, sr,
           e_core, e_rs, e_y, e_yr, e_ag, e_agc, l_core, l_rs, l_y, l_yr, l_x, l_ag, l_agc, l_agb, l_agbc):
    row, y = lax.axis_index("row"), lax.axis_index("col")
    px, pz, k = row // 8, (row // 2) % 4, row % 2
    qx = px + 1 - 2 * (px % 2)
    across, side = (row, 3 - y), (row, y + 1 - 2 * (y % 2))
    other = (row + 1 - 2 * k, y)

    def on_axis(h, c):
        return (jnp.where(h == 0, (c * 4 + pz) * 2 + k, (px * 4 + c) * 2 + k), y)

    def beside(d):
        return ((qx * 4 + pz) * 2 + k, (y + d) % 4)

    def first(h, x=px):
        return jnp.where(h == 0, x, pz)

    def second(h, x=px):
        return jnp.where(h == 0, pz, x)

    loads = [
        pltpu.make_async_copy(a_hbm.at[pl.ds(1024 * i, 1024)], own.at[pl.ds(1024 * i, 1024)], load_sem.at[i])
        for i in range(4)
    ]
    for c in loads:
        c.start()
    barrier = pltpu.get_barrier_semaphore()
    partners = [across, side, other] + [beside(d) for d in (1, 2, 3)]
    for d in (1, 2, 3):
        partners += [on_axis(0, (px + d) % 4), on_axis(1, (pz + d) % 4)]
    for p in partners:
        pl.semaphore_signal(barrier, inc=1, device_id=p, device_id_type=MESH)
    pl.semaphore_wait(barrier, len(partners))
    for c in loads:
        c.wait()

    def remote(src, dst, send, recv, to):
        return pltpu.make_async_remote_copy(
            src_ref=src, dst_ref=dst, send_sem=send, recv_sem=recv, device_id=to, device_id_type=MESH
        )

    def piece(j):
        return pl.ds(pl.multiple_of(j * CHUNK, CHUNK), CHUNK)

    def to_across(j):
        return remote(own.at[piece(j)], X.at[piece(j)], xs.at[j], xr.at[j], across)

    def to_side(j, src):
        return remote(src.at[piece(j)], S.at[piece(j)], ss.at[j], sr.at[j], side)

    def each(lo, hi, f):
        def step(j, _):
            f(j)
            return 0
        lax.fori_loop(lo, hi, step, 0)

    ahead = 8

    @pl.when(y >= 2)
    def _():
        each(EARLY, EARLY + ahead, lambda j: to_across(j).start())

    def forward(j):
        to_across(j).wait_recv()
        to_side(j, X).start()

        @pl.when(j < EARLY - ahead)
        def _():
            to_across(EARLY + j).wait_send()
            to_across(EARLY + ahead + j).start()

    def turned(j):
        return (j + EARLY) % PIECES

    def sided(j):
        return (y == 0) | (j < EARLY)

    def old_piece(j):
        to_across(j).wait_send()
        pl.when(sided(j))(lambda: to_side(turned(j), own).wait_send())

    def new_piece(j):
        pl.when(j >= LAG)(lambda: old_piece(j - LAG))
        to_across(j).start()
        pl.when(sided(j))(lambda: to_side(turned(j), own).start())

    sent, passed = [0], [0]

    def source(n):
        lo, hi = sent[0], min(sent[0] + n, PIECES)
        sent[0] = hi
        if hi > lo:
            pl.when(y < 2)(lambda: each(lo, hi, new_piece))

    def sink(n):
        lo, hi = passed[0], min(passed[0] + n, PIECES)
        passed[0] = hi
        if hi > lo:
            pl.when(y >= 2)(lambda: each(lo, hi, forward))

    def service(n):
        source(n)
        sink(n)

    def hooked(lo, past):
        def hook(p, b):
            j = 2 * p + b // 2
            pl.when((b % 2 == 1) & (y < 2) & (lo + j < PIECES))(lambda: new_piece(lo + j))
            pl.when((b % 2 == 1) & (y >= 2) & (past + j < PIECES))(lambda: forward(past + j))
        return hook

    base = pl.multiple_of(HALF * k, HALF)

    def lanes(h):
        return pl.ds(pl.multiple_of(HALF * h, HALF), HALF)

    def rows_a(h, c):
        return pl.ds(pl.multiple_of(base + 32 * c, 32), 32)

    def rows_b(h, c, x=px):
        return pl.ds(pl.multiple_of(base + 32 * first(h, x) + 8 * c, 8), 8)

    def exchange(make, n, pause):
        each(0, n, lambda j: make(j).start())
        pause()
        each(0, n, lambda j: make(j).wait())

    def scatter(ref, bc, ba, bb, sem_core, sem_rs, pauses):
        def halves(j):
            away = pl.ds(pl.multiple_of(HALF * (1 - k), HALF), HALF)
            return remote(ref.at[:, away], bc, sem_core.at[0], sem_core.at[1], other)

        def wide(j):
            h, d = j // 3, j % 3
            to = (first(h) + d + 1) % 4
            return remote(ref.at[:, rows_a(h, to), lanes(h)], ba.at[h, d],
                          sem_rs.at[0, 0, h, d], sem_rs.at[0, 1, h, d], on_axis(h, to))

        def narrow(j):
            h, d = j // 3, j % 3
            to = (second(h) + d + 1) % 4
            return remote(ref.at[:, rows_b(h, to), lanes(h)], bb.at[h, d],
                          sem_rs.at[1, 0, h, d], sem_rs.at[1, 1, h, d], on_axis(1 - h, to))

        exchange(halves, 1, pauses[0])
        ref[:, pl.ds(base, HALF), :] += bc[...]
        exchange(wide, 6, pauses[1])
        for h in (0, 1):
            ref[:, rows_a(h, first(h)), HALF * h : HALF * h + HALF] += (ba[h, 0] + ba[h, 1]) + ba[h, 2]
        exchange(narrow, 6, pauses[2])
        for h in (0, 1):
            ref[:, rows_b(h, second(h)), HALF * h : HALF * h + HALF] += (bb[h, 0] + bb[h, 1]) + bb[h, 2]

    def axis_part(ref, sem_ag, stage):
        def make(j):
            h, d = j // 3, j % 3
            if stage == 0:
                r, axis, coord = rows_b(h, second(h, qx), qx), 1 - h, second(h)
            else:
                r, axis, coord = rows_a(h, first(h, qx)), h, first(h)
            r = ref.at[:, r, lanes(h)]
            return remote(r, r, sem_ag.at[stage, 0, h, d], sem_ag.at[stage, 1, h, d],
                          on_axis(axis, (coord + d + 1) % 4))
        return make

    def core_part(ref, sem_core):
        r = ref.at[:, pl.ds(base, HALF)]
        return lambda j: remote(r, r, sem_core.at[0], sem_core.at[1], other)

    def mine(h, x=px):
        return rows_b(h, second(h, x), x), lanes(h)

    def group(g, ref):
        return ref[pl.ds(pl.multiple_of(g * GROUP, GROUP), GROUP), :]

    source(6)

    @pl.when(y < 2)
    def _():
        gown[...] = jnp.zeros_like(gown)

        def go(g):
            b = group(g, own)
            gown[0] += mm(b, b, 0, 0)
            pl.when(g % 8 == 7)(lambda: new_piece(6 + g // 8))
        each(0, ROWS // GROUP, go)
        sent[0] = 8
        scatter(gown, ec, ea, eb, e_core, e_rs, [lambda: source(1)] * 3)

    acc[...] = jnp.zeros_like(acc)

    def inner(g):
        def two(a, b, c):
            both = mm(jnp.concatenate([group(g, a), group(g, b)], axis=1), group(g, c), 0, 0)
            acc[1] += both[:PANEL]
            acc[2] += both[PANEL:]

        def one(a, b):
            acc[0] += mm(group(g, a), group(g, b), 0, 0)

        @pl.when(y == 0)
        def _():
            two(own, S, X)

        @pl.when(y == 1)
        def _():
            two(S, own, X)
            one(S, own)

        @pl.when(y == 2)
        def _():
            two(S, X, own)

        @pl.when(y == 3)
        def _():
            two(X, S, own)
            one(X, S)

    def shard_send(j):
        h, d = j // 4, j % 4
        return remote(gown.at[(0, *mine(h))], ge.at[(y, *mine(h))], e_y.at[h, d], e_yr.at[y, h], beside(d))

    pl.when(y < 2)(lambda: each(0, 8, lambda j: shard_send(j).start()))
    source(1)
    sink(2)
    QUARTER = EARLY // 4

    def step(i, _):
        @pl.when(y < 2)
        def _():
            new_piece(jnp.where(i == 3, 21, 12 + 2 * i))
            def got(j):
                to_across(j).wait_recv()
                to_side(j, own).wait_recv()
            each(EARLY + QUARTER * i, EARLY + QUARTER * i + QUARTER, got)
            each(8 + 2 * i, 10 + 2 * i, inner)
            pl.when(i < 2)(lambda: new_piece(13 + 2 * i))

        @pl.when(y >= 2)
        def _():
            pl.when(i == 0)(lambda: each(2, 4, forward))
            pl.when(i == 1)(lambda: forward(7))
            each(QUARTER * i, QUARTER * i + QUARTER, lambda j: to_side(j, X).wait_recv())
            each(2 * i, 2 * i + 2, inner)
            pl.when(i < 2)(lambda: each(4 * i + 4, 4 * i + 6, forward))
            pl.when(i == 2)(lambda: forward(12))

        @pl.when(i == 0)
        def _():
            pl.when(y < 2)(lambda: each(0, 8, lambda j: shard_send(j).wait_send()))

            def got(j):
                src, h = j // 2, j % 2
                v = ge.at[(src, *mine(h, qx))]
                remote(v, v, e_y.at[h, 0], e_yr.at[src, h], beside(0)).wait_recv()
            each(0, 4, got)
            exchange(axis_part(ge, e_ag, 0), 6, lambda: pl.when(y >= 2)(lambda: forward(6)))

        @pl.when(i == 1)
        def _():
            exchange(axis_part(ge, e_ag, 1), 6, lambda: pl.when(y >= 2)(lambda: forward(10)))
            exchange(core_part(ge, e_agc), 1, lambda: pl.when(y >= 2)(lambda: forward(11)))

        @pl.when(i == 2)
        def _():
            ge[...] = ge[...] * scale
            factor(ge.at[0], u1, sq.at[0], parts, us, ls, hooked(17, 13))
        return 0

    lax.fori_loop(0, 4, step, 0)
    sent[0], passed[0] = 22, 17
    sink(EXTRA)

    scatter(acc, lc, la, lb, l_core, l_rs, [lambda: service(1), lambda: service(2), lambda: service(1)])
    def swap(j):
        h, far = j // 2, j % 2
        r, c = mine(h)
        to = ((qx * 4 + pz) * 2 + k, jnp.where(far == 1, 3 - y, y))
        return remote(acc.at[pl.ds(1, 2), r, c], lx.at[far, h], l_x.at[0, far, h], l_x.at[1, far, h], to)

    def first_send(j):
        h, d = j // 4, j % 4
        return remote(acc.at[(0, *mine(h))], ly.at[y // 2, h], l_y.at[h, d], l_yr.at[y // 2, h], beside(d))

    pl.when(y % 2 == 1)(lambda: each(0, 8, lambda j: first_send(j).start()))
    each(0, 4, lambda j: swap(j).start())
    service(2)

    def got_first(j):
        src, h = j // 2, j % 2
        v = acc.at[(0, *mine(h))]
        remote(v, ly.at[src, h], l_y.at[h, 0], l_yr.at[src, h], beside(0)).wait_recv()
    each(0, 4, got_first)
    each(0, 4, lambda j: swap(j).wait())
    for h in (0, 1):
        r, c = mine(h, qx)
        gl[0, r, c] = ly[0, h] + ly[1, h]
        gl[1:3, r, c] = lx[0, h] + lx[1, h]
    exchange(axis_part(gl, l_ag, 0), 6, lambda: service(1))
    lead, others = gl.at[pl.ds(0, 1)], gl.at[pl.ds(1, 2)]
    wide, late_wide = axis_part(lead, l_ag, 1), axis_part(others, l_agb, 1)
    late_core = core_part(others, l_agbc)
    each(0, 6, lambda j: wide(j).start())
    each(0, 6, lambda j: late_wide(j).start())
    service(2)
    each(0, 6, lambda j: wide(j).wait())
    exchange(core_part(lead, l_agc), 1, lambda: service(1))

    sq[1] = ge[1]
    sq[2] = gl[0] * scale

    def pick(i, a, b, c, d):
        return jnp.where(i == 0, a, jnp.where(i == 1, b, jnp.where(i == 2, c, d)))

    def products(i, _):
        @pl.when((i == 0) | (y >= 2))
        def _():
            p = mm(sq[pick(i, 0, 0, 5, 6)], sq[pick(i, 2, 3, 10, 11)])
            p = jnp.where(i == 3, sq[7] - p, p)
            sq[pick(i, 6, 7, 8, 12)] = p
            q = mm(sq[pick(i, 6, 6, 5, 0)], p, 0, 0)
            q = jnp.where(i < 2, sq[pick(i, 1, 4, 4, 4)] - q, q)
            sq[pick(i, 9, 10, 11, 13)] = q

        @pl.when(i == 0)
        def _():
            each(0, 6, lambda j: late_wide(j).wait())
            late_core(0).start()
            factor(sq.at[9], u2, sq.at[5], parts, us, ls, hooked(sent[0], passed[0]))
            late_core(0).wait()
            sq[3] = gl[1] * scale
            sq[4] = gl[2] * scale
        return 0

    lax.fori_loop(0, 4, products, 0)
    sent[0], passed[0] = min(sent[0] + 4, PIECES), min(passed[0] + 4, PIECES)
    source(PIECES)

    @pl.when(y == 0)
    def _():
        m1[...] = sq[0].T

    @pl.when(y == 1)
    def _():
        m1[...] = sq[5].T
        m2[...] = -mm(mm(sq[0], sq[6], 0, 0), m1[...])

    @pl.when(y >= 2)
    def _():
        m1[...] = -sq[jnp.where(y == 2, 11, 13)]
        m2[...] = -sq[jnp.where(y == 2, 13, 11)]

    @pl.when(y == 0)
    def _():
        mcat[: len(TERMS) * PANEL] = stacked([three(m1[...])], 1, 0)

    @pl.when(y >= 1)
    def _():
        mcat[...] = stacked([three(m1[...]), three(m2[...])], 1, 0)

    per = APPLY // CHUNK
    steps = ROWS // APPLY

    def part(g):
        return pl.ds(pl.multiple_of(g * APPLY, APPLY), APPLY)

    def store(g):
        return pltpu.make_async_copy(out.at[part(g)], out_hbm.at[part(g)], out_sem.at[g])

    @pl.when(y == 0)
    def _():
        def go(g):
            a = stacked([three(own[part(g), :])], 0, 1)
            out[part(g), :] = jnp.dot(a, mcat[: len(TERMS) * PANEL], preferred_element_type=F32)
            store(g).start()
        each(0, steps, go)

    @pl.when(y == 1)
    def _():
        def go(i):
            g = (i + steps // 2) % steps
            pl.when(g < steps // 2)(lambda: each(per * g, per * g + per, lambda j: to_side(j, own).wait_recv()))
            a = stacked([three(own[part(g), :]), three(S[part(g), :])], 0, 1)
            out[part(g), :] = jnp.dot(a, mcat[...], preferred_element_type=F32)
            store(g).start()
        each(0, steps, go)

    done = passed[0]

    @pl.when(y >= 2)
    def _():
        def reach(g):
            return jnp.minimum(jnp.maximum(done + g, per * g + per), PIECES)
        def go(g):
            each(jnp.where(g == 0, done, reach(g - 1)), reach(g), forward)
            pl.when(g >= steps // 2)(lambda: each(per * g, per * g + per, lambda j: to_side(j, X).wait_recv()))
            a = stacked([three(X[part(g), :]), three(S[part(g), :])], 0, 1)
            out[part(g), :] = own[part(g), :] + jnp.dot(a, mcat[...], preferred_element_type=F32)
            store(g).start()
        each(0, steps, go)

    @pl.when(y == 0)
    def _():
        upper_ref[:PANEL] = u1[...]
        upper_ref[PANEL:] = jnp.zeros((PANEL, PANEL), F32)

    @pl.when(y == 1)
    def _():
        upper_ref[:PANEL] = sq[6]
        upper_ref[PANEL:] = u2[...]

    @pl.when(y >= 2)
    def _():
        upper_ref[:PANEL] = sq[7]
        upper_ref[PANEL:] = sq[8]

    pl.when(y % 2 == 1)(lambda: each(0, 8, lambda j: first_send(j).wait_send()))

    @pl.when(y < 2)
    def _():
        each(PIECES - LAG, PIECES, old_piece)

    @pl.when(y >= 2)
    def _():
        each(PIECES - ahead, PIECES, lambda j: to_across(j).wait_send())
        each(0, PIECES, lambda j: to_side(j, X).wait_send())

    each(0, steps, lambda g: store(g).wait())


def on_device(total_rows, influence):
    vmem = lambda *s: pltpu.VMEM(s, F32)
    dma = lambda *s: pltpu.SemaphoreType.DMA(s)
    block = vmem(PANEL, PANEL)
    factored, upper = pl.pallas_call(
        functools.partial(kernel, 1.0 / total_rows),
        name="factor_panels",
        out_shape=[jax.ShapeDtypeStruct((ROWS, PANEL), F32), jax.ShapeDtypeStruct((2 * PANEL, PANEL), F32)],
        in_specs=[pl.BlockSpec(memory_space=pl.ANY)],
        out_specs=[pl.BlockSpec(memory_space=pl.ANY)] + [pl.BlockSpec(memory_space=pltpu.VMEM)],
        scratch_shapes=[
            vmem(ROWS, PANEL), vmem(ROWS, PANEL), vmem(ROWS, PANEL), vmem(ROWS, PANEL),
            vmem(1, PANEL, PANEL), vmem(2, PANEL, PANEL), vmem(3, PANEL, PANEL), vmem(3, PANEL, PANEL),
            block, block, block, block, pltpu.VMEM((2 * len(TERMS) * PANEL, PANEL), BF16), vmem(14, PANEL, PANEL),
            vmem(2, HALF, HALF), vmem(2, HALF, HALF), vmem(2, HALF, HALF),
            vmem(1, HALF, PANEL), vmem(2, 3, 1, 32, HALF), vmem(2, 3, 1, 8, HALF),
            vmem(3, HALF, PANEL), vmem(2, 3, 3, 32, HALF), vmem(2, 3, 3, 8, HALF),
            vmem(2, 2, 8, HALF), vmem(2, 2, 2, 8, HALF),
            dma(4), dma(ROWS // APPLY), dma(PIECES), dma(PIECES), dma(PIECES), dma(PIECES),
            dma(2), dma(2, 2, 2, 3), dma(2, 4), dma(2, 2), dma(2, 2, 2, 3), dma(2),
            dma(2), dma(2, 2, 2, 3), dma(2, 4), dma(2, 2), dma(2, 2, 2), dma(2, 2, 2, 3), dma(2),
            dma(2, 2, 2, 3), dma(2),
        ],
        compiler_params=pltpu.CompilerParams(
            collective_id=0, has_side_effects=True, vmem_limit_bytes=56 * 2**20
        ),
    )(influence)
    return factored, upper


def solution(mesh):
    total_rows = ROWS * mesh.shape["row"]
    return jax.shard_map(
        functools.partial(on_device, total_rows),
        mesh=mesh,
        in_specs=(P("row", "col"),),
        out_specs=(P("row", "col"), P(None, "col")),
        check_vma=False,
    )
```

```python
import functools

import jax
import jax.numpy as jnp
from jax import lax
from jax.experimental import pallas as pl
from jax.experimental.pallas import tpu as pltpu
from jax.sharding import PartitionSpec as P

MESH = pl.DeviceIdType.MESH
F32 = jnp.float32
PANEL = 256
HALF = 128
ROWS = 4096
CHUNK = 128
PIECES = ROWS // CHUNK
EARLY = PIECES // 2
GROUP = 256
EXTRA = 1
LAG = 6
APPLY = 512


def mm(a, b, ca=1, cb=0):
    return lax.dot_general(
        a, b, (((ca,), (cb,)), ((), ())),
        precision=lax.Precision.HIGHEST, preferred_element_type=F32,
    )


BF16 = jnp.bfloat16
TERMS = ((2, 0), (0, 2), (1, 1), (1, 0), (0, 1), (0, 0))


def three(a):
    high = a.astype(BF16)
    rest = a - high.astype(F32)
    middle = rest.astype(BF16)
    return high, middle, (rest - middle.astype(F32)).astype(BF16)


def stacked(parts_of, side, axis):
    return jnp.concatenate([p[t[side]] for t in TERMS for p in parts_of], axis=axis)


def spread(v):
    return jnp.broadcast_to(v, (8, HALF))


def eliminate(square, u_ref, li_ref, hook, nb=4):
    sub = lax.broadcasted_iota(jnp.int32, (8, HALF), 0)
    lane = lax.broadcasted_iota(jnp.int32, (8, HALF), 1)
    zero = jnp.zeros((8, HALF), F32)
    tiles = HALF // 8
    left = tuple(square[8 * i : 8 * i + 8, :] for i in range(tiles))
    right = tuple(jnp.where(lane == sub + 8 * i, 1.0, 0.0).astype(F32) for i in range(tiles))

    def eight(left, right, q):
        w = [spread(left[0][:, 8 * q + m : 8 * q + m + 1]) for m in range(8)] + [left[0], right[0]]
        rows = [zero, zero]
        for j in range(0, 8, 2):
            pivot = (sub == j) | (sub == j + 1)
            p00, p01, p11 = spread(w[j][j : j + 1]), spread(w[j][j + 1 : j + 2]), spread(w[j + 1][j + 1 : j + 2])
            rd = 1.0 / (p00 * p11 - p01 * p01)
            i00, i01, i11 = p11 * rd, p01 * rd, p00 * rd
            u, v = jnp.where(pivot, 0.0, w[j]), jnp.where(pivot, 0.0, w[j + 1])
            s0 = lax.rsqrt(p00)
            m0 = p01 * (s0 * s0)
            s1 = lax.rsqrt(p11 - m0 * p01)
            for t in list(range(j + 2, 8)) + [8, 9]:
                r0, r1 = spread(w[t][j : j + 1]), spread(w[t][j + 1 : j + 2])
                a, b = r0 * i00 - r1 * i01, r1 * i11 - r0 * i01
                if t >= 8:
                    rows[t - 8] = jnp.where(
                        sub == j, r0 * s0, jnp.where(sub == j + 1, (r1 - m0 * r0) * s1, rows[t - 8])
                    )
                w[t] = jnp.where(sub == j, a, jnp.where(sub == j + 1, b, w[t] - (u * a + v * b)))
        ql = [spread(w[8][m : m + 1]) for m in range(8)]
        qr = [spread(w[9][m : m + 1]) for m in range(8)]

        def total(c, q):
            t = [c[m] * q[m] for m in range(8)]
            return ((t[0] + t[1]) + (t[2] + t[3])) + ((t[4] + t[5]) + (t[6] + t[7]))

        for i in range(1, tiles):
            c = [spread(left[i][:, 8 * q + m : 8 * q + m + 1]) for m in range(8)]
            left[i] = left[i] - total(c, ql)
            right[i] = right[i] - total(c, qr)
        return rows

    def body(b, carry):
        left, right = list(carry[0]), list(carry[1])
        for q in range(nb):
            up, low = eight(left, right, q)
            r = pl.ds(pl.multiple_of(8 * (b * nb + q), 8), 8)
            up = jnp.where(lane >= sub + 8 * q, up, 0.0)
            u_ref[r, :] = pltpu.roll(up, 8 * nb * b, 1)
            li_ref[r, :] = low
            left, right = left[1:] + [zero], right[1:] + [zero]
        left = [pltpu.roll(t, HALF - 8 * nb, 1) for t in left]
        hook(b)
        return tuple(left), tuple(right)

    lax.fori_loop(0, tiles // nb, body, (left, right))


HEAD, TAIL = slice(0, HALF), slice(HALF, PANEL)


def factor(g_ref, u_ref, li_ref, parts, us, ls, hook):
    parts[0] = g_ref[HEAD, HEAD]

    def block(p, _):
        eliminate(parts[p], us.at[p], ls.at[p], functools.partial(hook, p))

        @pl.when(p == 0)
        def _():
            l11 = ls[0]
            u12 = mm(l11, g_ref[HEAD, TAIL])
            u_ref[HEAD, TAIL] = u12
            parts[1] = g_ref[TAIL, TAIL] - mm(u12, u12, 0, 0)
            li_ref[TAIL, HEAD] = mm(u12, l11, 0, 0)
        return 0

    lax.fori_loop(0, 2, block, 0)
    li_ref[TAIL, HEAD] = -mm(ls[1], li_ref[TAIL, HEAD])
    for p, c in ((0, HEAD), (1, TAIL)):
        u_ref[c, c] = us[p]
        li_ref[c, c] = ls[p]
    u_ref[TAIL, HEAD] = jnp.zeros((HALF, HALF), F32)
    li_ref[HEAD, TAIL] = jnp.zeros((HALF, HALF), F32)


def kernel(scale, a_hbm, out_hbm, upper_ref,
           own, X, S, out, gown, ge, acc, accs, gl, u1, u2, m1, m2, mcat, sq, parts, us, ls,
           ec, ea, eb, lc, la, lb, mc, ma, mb, ly, lx,
           load_sem, out_sem, xs, xr, ss, sr,
           e_core, e_rs, e_y, e_yr, e_ag, e_agc, l_core, l_rs, l_y, l_yr, l_x, l_ag, l_agc, l_agb, l_agbc, m_core, m_rs):
    row, y = lax.axis_index("row"), lax.axis_index("col")
    px, pz, k = row // 8, (row // 2) % 4, row % 2
    qx = px + 1 - 2 * (px % 2)
    across, side = (row, 3 - y), (row, y + 1 - 2 * (y % 2))
    other = (row + 1 - 2 * k, y)

    def on_axis(h, c):
        return (jnp.where(h == 0, (c * 4 + pz) * 2 + k, (px * 4 + c) * 2 + k), y)

    def beside(d):
        return ((qx * 4 + pz) * 2 + k, (y + d) % 4)

    def first(h, x=px):
        return jnp.where(h == 0, x, pz)

    def second(h, x=px):
        return jnp.where(h == 0, pz, x)

    loads = [
        pltpu.make_async_copy(a_hbm.at[pl.ds(1024 * i, 1024)], own.at[pl.ds(1024 * i, 1024)], load_sem.at[i])
        for i in range(4)
    ]
    for c in loads:
        c.start()
    barrier = pltpu.get_barrier_semaphore()
    partners = [across, side, other] + [beside(d) for d in (1, 2, 3)]
    for d in (1, 2, 3):
        partners += [on_axis(0, (px + d) % 4), on_axis(1, (pz + d) % 4)]
    for p in partners:
        pl.semaphore_signal(barrier, inc=1, device_id=p, device_id_type=MESH)
    pl.semaphore_wait(barrier, len(partners))
    for c in loads:
        c.wait()

    def remote(src, dst, send, recv, to):
        return pltpu.make_async_remote_copy(
            src_ref=src, dst_ref=dst, send_sem=send, recv_sem=recv, device_id=to, device_id_type=MESH
        )

    def piece(j):
        return pl.ds(pl.multiple_of(j * CHUNK, CHUNK), CHUNK)

    def to_across(j):
        return remote(own.at[piece(j)], X.at[piece(j)], xs.at[j], xr.at[j], across)

    def to_side(j, src):
        return remote(src.at[piece(j)], S.at[piece(j)], ss.at[j], sr.at[j], side)

    def each(lo, hi, f):
        def step(j, _):
            f(j)
            return 0
        lax.fori_loop(lo, hi, step, 0)

    ahead = 8

    @pl.when(y >= 2)
    def _():
        each(EARLY, EARLY + ahead, lambda j: to_across(j).start())

    def forward(j):
        to_across(j).wait_recv()
        to_side(j, X).start()

        @pl.when(j < EARLY - ahead)
        def _():
            to_across(EARLY + j).wait_send()
            to_across(EARLY + ahead + j).start()

    def turned(j):
        return (j + EARLY) % PIECES

    def sided(j):
        return (y == 0) | (j < EARLY)

    def old_piece(j):
        to_across(j).wait_send()
        pl.when(sided(j))(lambda: to_side(turned(j), own).wait_send())

    def new_piece(j):
        pl.when(j >= LAG)(lambda: old_piece(j - LAG))
        to_across(j).start()
        pl.when(sided(j))(lambda: to_side(turned(j), own).start())

    sent, passed = [0], [0]

    def source(n):
        lo, hi = sent[0], min(sent[0] + n, PIECES)
        sent[0] = hi
        if hi > lo:
            pl.when(y < 2)(lambda: each(lo, hi, new_piece))

    def sink(n):
        lo, hi = passed[0], min(passed[0] + n, PIECES)
        passed[0] = hi
        if hi > lo:
            pl.when(y >= 2)(lambda: each(lo, hi, forward))

    def service(n):
        source(n)
        sink(n)

    def hooked(lo, past):
        def hook(p, b):
            j = 2 * p + b // 2
            pl.when((b % 2 == 1) & (y < 2) & (lo + j < PIECES))(lambda: new_piece(lo + j))
            pl.when((b % 2 == 1) & (y >= 2) & (past + j < PIECES))(lambda: forward(past + j))
        return hook

    base = pl.multiple_of(HALF * k, HALF)

    def lanes(h):
        return pl.ds(pl.multiple_of(HALF * h, HALF), HALF)

    def rows_a(h, c):
        return pl.ds(pl.multiple_of(base + 32 * c, 32), 32)

    def rows_b(h, c, x=px):
        return pl.ds(pl.multiple_of(base + 32 * first(h, x) + 8 * c, 8), 8)

    def exchange(make, n, pause):
        each(0, n, lambda j: make(j).start())
        pause()
        each(0, n, lambda j: make(j).wait())

    def scatter(ref, bc, ba, bb, sem_core, sem_rs):
        def halves(j):
            away = pl.ds(pl.multiple_of(HALF * (1 - k), HALF), HALF)
            return remote(ref.at[:, away], bc, sem_core.at[0], sem_core.at[1], other)

        def wide(j):
            h, d = j // 3, j % 3
            to = (first(h) + d + 1) % 4
            return remote(ref.at[:, rows_a(h, to), lanes(h)], ba.at[h, d],
                          sem_rs.at[0, 0, h, d], sem_rs.at[0, 1, h, d], on_axis(h, to))

        def narrow(j):
            h, d = j // 3, j % 3
            to = (second(h) + d + 1) % 4
            return remote(ref.at[:, rows_b(h, to), lanes(h)], bb.at[h, d],
                          sem_rs.at[1, 0, h, d], sem_rs.at[1, 1, h, d], on_axis(1 - h, to))

        def add_half():
            ref[:, pl.ds(base, HALF), :] += bc[...]

        def add_wide():
            for h in (0, 1):
                ref[:, rows_a(h, first(h)), HALF * h : HALF * h + HALF] += (ba[h, 0] + ba[h, 1]) + ba[h, 2]

        def add_narrow():
            for h in (0, 1):
                ref[:, rows_b(h, second(h)), HALF * h : HALF * h + HALF] += (bb[h, 0] + bb[h, 1]) + bb[h, 2]

        return (halves, 1, add_half), (wide, 6, add_wide), (narrow, 6, add_narrow)

    def begin(stage):
        each(0, stage[1], lambda j: stage[0](j).start())

    def finish(stage):
        each(0, stage[1], lambda j: stage[0](j).wait())
        stage[2]()

    def axis_part(ref, sem_ag, stage):
        def make(j):
            h, d = j // 3, j % 3
            if stage == 0:
                r, axis, coord = rows_b(h, second(h, qx), qx), 1 - h, second(h)
            else:
                r, axis, coord = rows_a(h, first(h, qx)), h, first(h)
            r = ref.at[:, r, lanes(h)]
            return remote(r, r, sem_ag.at[stage, 0, h, d], sem_ag.at[stage, 1, h, d],
                          on_axis(axis, (coord + d + 1) % 4))
        return make

    def core_part(ref, sem_core):
        r = ref.at[:, pl.ds(base, HALF)]
        return lambda j: remote(r, r, sem_core.at[0], sem_core.at[1], other)

    def mine(h, x=px):
        return rows_b(h, second(h, x), x), lanes(h)

    def group(g, ref):
        return ref[pl.ds(pl.multiple_of(g * GROUP, GROUP), GROUP), :]

    source(6)

    @pl.when(y < 2)
    def _():
        gown[...] = jnp.zeros_like(gown)

        def go(g):
            b = group(g, own)
            gown[0] += mm(b, b, 0, 0)
            pl.when(g % 8 == 7)(lambda: new_piece(6 + g // 8))
        each(0, ROWS // GROUP, go)
        sent[0] = 8
        for stage in scatter(gown, ec, ea, eb, e_core, e_rs):
            begin(stage)
            source(1)
            finish(stage)

    acc[...] = jnp.zeros_like(acc)
    accs[...] = jnp.zeros_like(accs)

    def inner(g):
        def two(a, b, c):
            both = mm(jnp.concatenate([group(g, a), group(g, b)], axis=1), group(g, c), 0, 0)
            accs[0] += both[:PANEL]
            accs[1] += both[PANEL:]

        def one(a, b):
            acc[0] += mm(group(g, a), group(g, b), 0, 0)

        @pl.when(y == 0)
        def _():
            two(own, S, X)

        @pl.when(y == 1)
        def _():
            two(S, own, X)
            one(S, own)

        @pl.when(y == 2)
        def _():
            two(S, X, own)

        @pl.when(y == 3)
        def _():
            two(X, S, own)
            one(X, S)

    def shard_send(j):
        h, d = j // 4, j % 4
        return remote(gown.at[(0, *mine(h))], ge.at[(y, *mine(h))], e_y.at[h, d], e_yr.at[y, h], beside(d))

    pl.when(y < 2)(lambda: each(0, 8, lambda j: shard_send(j).start()))
    source(1)
    sink(2)
    QUARTER = EARLY // 4

    def step(i, _):
        @pl.when(y < 2)
        def _():
            new_piece(jnp.where(i == 3, 21, 12 + 2 * i))
            def got(j):
                to_across(j).wait_recv()
                to_side(j, own).wait_recv()
            each(EARLY + QUARTER * i, EARLY + QUARTER * i + QUARTER, got)
            each(8 + 2 * i, 10 + 2 * i, inner)
            pl.when(i < 2)(lambda: new_piece(13 + 2 * i))

        @pl.when(y >= 2)
        def _():
            pl.when(i == 0)(lambda: each(2, 4, forward))
            pl.when(i == 1)(lambda: forward(7))
            each(QUARTER * i, QUARTER * i + QUARTER, lambda j: to_side(j, X).wait_recv())
            each(2 * i, 2 * i + 2, inner)
            pl.when(i < 2)(lambda: each(4 * i + 4, 4 * i + 6, forward))
            pl.when(i == 2)(lambda: forward(12))

        @pl.when(i == 0)
        def _():
            pl.when(y < 2)(lambda: each(0, 8, lambda j: shard_send(j).wait_send()))

            def got(j):
                src, h = j // 2, j % 2
                v = ge.at[(src, *mine(h, qx))]
                remote(v, v, e_y.at[h, 0], e_yr.at[src, h], beside(0)).wait_recv()
            each(0, 4, got)
            exchange(axis_part(ge, e_ag, 0), 6, lambda: pl.when(y >= 2)(lambda: forward(6)))

        @pl.when(i == 1)
        def _():
            exchange(axis_part(ge, e_ag, 1), 6, lambda: pl.when(y >= 2)(lambda: forward(10)))
            exchange(core_part(ge, e_agc), 1, lambda: pl.when(y >= 2)(lambda: forward(11)))

        @pl.when(i == 2)
        def _():
            ge[...] = ge[...] * scale
            factor(ge.at[0], u1, sq.at[0], parts, us, ls, hooked(17, 13))
        return 0

    lax.fori_loop(0, 4, step, 0)
    sent[0], passed[0] = 22, 17
    sink(EXTRA)

    lead = scatter(acc, lc, la, lb, l_core, l_rs)
    rest = scatter(accs, mc, ma, mb, m_core, m_rs)
    begin(lead[0])
    begin(rest[0])
    for n, pieces in ((0, 1), (1, 2)):
        service(pieces)
        finish(lead[n])
        begin(lead[n + 1])
        finish(rest[n])
        begin(rest[n + 1])
    service(1)
    finish(lead[2])

    def swap(j):
        h, far = j // 2, j % 2
        r, c = mine(h)
        to = ((qx * 4 + pz) * 2 + k, jnp.where(far == 1, 3 - y, y))
        return remote(accs.at[:, r, c], lx.at[far, h], l_x.at[0, far, h], l_x.at[1, far, h], to)

    def first_send(j):
        h, d = j // 4, j % 4
        return remote(acc.at[(0, *mine(h))], ly.at[y // 2, h], l_y.at[h, d], l_yr.at[y // 2, h], beside(d))

    pl.when(y % 2 == 1)(lambda: each(0, 8, lambda j: first_send(j).start()))
    finish(rest[2])
    each(0, 4, lambda j: swap(j).start())
    service(2)

    def got_first(j):
        src, h = j // 2, j % 2
        v = acc.at[(0, *mine(h))]
        remote(v, ly.at[src, h], l_y.at[h, 0], l_yr.at[src, h], beside(0)).wait_recv()
    each(0, 4, got_first)
    for h in (0, 1):
        r, c = mine(h, qx)
        gl[0, r, c] = ly[0, h] + ly[1, h]
    front, others = gl.at[pl.ds(0, 1)], gl.at[pl.ds(1, 2)]
    near, wide = axis_part(front, l_ag, 0), axis_part(front, l_ag, 1)
    late_near, late_wide = axis_part(others, l_agb, 0), axis_part(others, l_agb, 1)
    late_core = core_part(others, l_agbc)
    each(0, 6, lambda j: near(j).start())
    each(0, 4, lambda j: swap(j).wait())
    for h in (0, 1):
        r, c = mine(h, qx)
        gl[1:3, r, c] = lx[0, h] + lx[1, h]
    each(0, 6, lambda j: late_near(j).start())
    service(1)
    each(0, 6, lambda j: near(j).wait())
    each(0, 6, lambda j: wide(j).start())
    each(0, 6, lambda j: late_near(j).wait())
    each(0, 6, lambda j: late_wide(j).start())
    service(2)
    each(0, 6, lambda j: wide(j).wait())
    exchange(core_part(front, l_agc), 1, lambda: service(1))

    sq[1] = ge[1]
    sq[2] = gl[0] * scale

    def pick(i, a, b, c, d):
        return jnp.where(i == 0, a, jnp.where(i == 1, b, jnp.where(i == 2, c, d)))

    def products(i, _):
        @pl.when((i == 0) | (y >= 2))
        def _():
            p = mm(sq[pick(i, 0, 0, 5, 6)], sq[pick(i, 2, 3, 10, 11)])
            p = jnp.where(i == 3, sq[7] - p, p)
            sq[pick(i, 6, 7, 8, 12)] = p
            q = mm(sq[pick(i, 6, 6, 5, 0)], p, 0, 0)
            q = jnp.where(i < 2, sq[pick(i, 1, 4, 4, 4)] - q, q)
            sq[pick(i, 9, 10, 11, 13)] = q

        @pl.when(i == 0)
        def _():
            each(0, 6, lambda j: late_wide(j).wait())
            late_core(0).start()
            factor(sq.at[9], u2, sq.at[5], parts, us, ls, hooked(sent[0], passed[0]))
            late_core(0).wait()
            sq[3] = gl[1] * scale
            sq[4] = gl[2] * scale
        return 0

    lax.fori_loop(0, 4, products, 0)
    sent[0], passed[0] = min(sent[0] + 4, PIECES), min(passed[0] + 4, PIECES)
    source(PIECES)

    @pl.when(y == 0)
    def _():
        m1[...] = sq[0].T

    @pl.when(y == 1)
    def _():
        m1[...] = sq[5].T
        m2[...] = -mm(mm(sq[0], sq[6], 0, 0), m1[...])

    @pl.when(y >= 2)
    def _():
        m1[...] = -sq[jnp.where(y == 2, 11, 13)]
        m2[...] = -sq[jnp.where(y == 2, 13, 11)]

    @pl.when(y == 0)
    def _():
        mcat[: len(TERMS) * PANEL] = stacked([three(m1[...])], 1, 0)

    @pl.when(y >= 1)
    def _():
        mcat[...] = stacked([three(m1[...]), three(m2[...])], 1, 0)

    per = APPLY // CHUNK
    steps = ROWS // APPLY

    def part(g):
        return pl.ds(pl.multiple_of(g * APPLY, APPLY), APPLY)

    def store(g):
        return pltpu.make_async_copy(out.at[part(g)], out_hbm.at[part(g)], out_sem.at[g])

    @pl.when(y == 0)
    def _():
        def go(g):
            a = stacked([three(own[part(g), :])], 0, 1)
            out[part(g), :] = jnp.dot(a, mcat[: len(TERMS) * PANEL], preferred_element_type=F32)
            store(g).start()
        each(0, steps, go)

    @pl.when(y == 1)
    def _():
        def go(i):
            g = (i + steps // 2) % steps
            pl.when(g < steps // 2)(lambda: each(per * g, per * g + per, lambda j: to_side(j, own).wait_recv()))
            a = stacked([three(own[part(g), :]), three(S[part(g), :])], 0, 1)
            out[part(g), :] = jnp.dot(a, mcat[...], preferred_element_type=F32)
            store(g).start()
        each(0, steps, go)

    done = passed[0]

    @pl.when(y >= 2)
    def _():
        def reach(g):
            return jnp.minimum(jnp.maximum(done + g, per * g + per), PIECES)
        def go(g):
            each(jnp.where(g == 0, done, reach(g - 1)), reach(g), forward)
            pl.when(g >= steps // 2)(lambda: each(per * g, per * g + per, lambda j: to_side(j, X).wait_recv()))
            a = stacked([three(X[part(g), :]), three(S[part(g), :])], 0, 1)
            out[part(g), :] = own[part(g), :] + jnp.dot(a, mcat[...], preferred_element_type=F32)
            store(g).start()
        each(0, steps, go)

    @pl.when(y == 0)
    def _():
        upper_ref[:PANEL] = u1[...]
        upper_ref[PANEL:] = jnp.zeros((PANEL, PANEL), F32)

    @pl.when(y == 1)
    def _():
        upper_ref[:PANEL] = sq[6]
        upper_ref[PANEL:] = u2[...]

    @pl.when(y >= 2)
    def _():
        upper_ref[:PANEL] = sq[7]
        upper_ref[PANEL:] = sq[8]

    pl.when(y % 2 == 1)(lambda: each(0, 8, lambda j: first_send(j).wait_send()))

    @pl.when(y < 2)
    def _():
        each(PIECES - LAG, PIECES, old_piece)

    @pl.when(y >= 2)
    def _():
        each(PIECES - ahead, PIECES, lambda j: to_across(j).wait_send())
        each(0, PIECES, lambda j: to_side(j, X).wait_send())

    each(0, steps, lambda g: store(g).wait())


PLACED = 4


def place(a_ref, b_ref, out_ref, upper_ref, a_buf, b_buf, sems):
    step = ROWS // PLACED
    pairs = [(a_ref.at[pl.ds(i * step, step)], a_buf.at[pl.ds(i * step, step)], out_ref.at[pl.ds(i * step, step)])
             for i in range(PLACED)] + [(b_ref, b_buf, upper_ref)]
    ins = [pltpu.make_async_copy(s, b, sems.at[0, i]) for i, (s, b, _) in enumerate(pairs)]
    outs = [pltpu.make_async_copy(b, d, sems.at[1, i]) for i, (_, b, d) in enumerate(pairs)]
    for c in ins:
        c.start()
    for c, d in zip(ins, outs):
        c.wait()
        d.start()
    for d in outs:
        d.wait()


def on_device(total_rows, influence):
    vmem = lambda *s: pltpu.VMEM(s, F32)
    dma = lambda *s: pltpu.SemaphoreType.DMA(s)
    block = vmem(PANEL, PANEL)
    factored, upper = pl.pallas_call(
        functools.partial(kernel, 1.0 / total_rows),
        name="factor_panels",
        out_shape=[jax.ShapeDtypeStruct((ROWS, PANEL), F32), jax.ShapeDtypeStruct((2 * PANEL, PANEL), F32)],
        in_specs=[pl.BlockSpec(memory_space=pl.ANY)],
        out_specs=[pl.BlockSpec(memory_space=pl.ANY)] + [pl.BlockSpec(memory_space=pltpu.VMEM)],
        scratch_shapes=[
            vmem(ROWS, PANEL), vmem(ROWS, PANEL), vmem(ROWS, PANEL), vmem(ROWS, PANEL),
            vmem(1, PANEL, PANEL), vmem(2, PANEL, PANEL), vmem(1, PANEL, PANEL), vmem(2, PANEL, PANEL),
            vmem(3, PANEL, PANEL),
            block, block, block, block, pltpu.VMEM((2 * len(TERMS) * PANEL, PANEL), BF16), vmem(14, PANEL, PANEL),
            vmem(2, HALF, HALF), vmem(2, HALF, HALF), vmem(2, HALF, HALF),
            vmem(1, HALF, PANEL), vmem(2, 3, 1, 32, HALF), vmem(2, 3, 1, 8, HALF),
            vmem(1, HALF, PANEL), vmem(2, 3, 1, 32, HALF), vmem(2, 3, 1, 8, HALF),
            vmem(2, HALF, PANEL), vmem(2, 3, 2, 32, HALF), vmem(2, 3, 2, 8, HALF),
            vmem(2, 2, 8, HALF), vmem(2, 2, 2, 8, HALF),
            dma(4), dma(ROWS // APPLY), dma(PIECES), dma(PIECES), dma(PIECES), dma(PIECES),
            dma(2), dma(2, 2, 2, 3), dma(2, 4), dma(2, 2), dma(2, 2, 2, 3), dma(2),
            dma(2), dma(2, 2, 2, 3), dma(2, 4), dma(2, 2), dma(2, 2, 2), dma(2, 2, 2, 3), dma(2),
            dma(2, 2, 2, 3), dma(2), dma(2), dma(2, 2, 2, 3),
        ],
        compiler_params=pltpu.CompilerParams(
            collective_id=0, has_side_effects=True, vmem_limit_bytes=56 * 2**20
        ),
    )(influence)
    return pl.pallas_call(
        place,
        name="place_results",
        out_shape=[jax.ShapeDtypeStruct((ROWS, PANEL), F32), jax.ShapeDtypeStruct((2 * PANEL, PANEL), F32)],
        in_specs=[pl.BlockSpec(memory_space=pl.ANY)] * 2,
        out_specs=[pl.BlockSpec(memory_space=pl.ANY)] * 2,
        scratch_shapes=[vmem(ROWS, PANEL), vmem(2 * PANEL, PANEL), dma(2, PLACED + 1)],
        compiler_params=pltpu.CompilerParams(vmem_limit_bytes=60 * 2**20),
    )(factored, upper)


def solution(mesh):
    total_rows = ROWS * mesh.shape["row"]
    return jax.shard_map(
        functools.partial(on_device, total_rows),
        mesh=mesh,
        in_specs=(P("row", "col"),),
        out_specs=(P("row", "col"), P(None, "col")),
        check_vma=False,
    )
```

```python
import functools

import jax
import jax.numpy as jnp
from jax import lax
from jax.experimental import pallas as pl
from jax.experimental.pallas import tpu as pltpu
from jax.sharding import PartitionSpec as P

MESH = pl.DeviceIdType.MESH
F32 = jnp.float32
PANEL = 256
HALF = 128
ROWS = 4096
CHUNK = 128
PIECES = ROWS // CHUNK
EARLY = PIECES // 2
GROUP = 256
LAG = 6
APPLY = 512


def mm(a, b, ca=1, cb=0):
    return lax.dot_general(
        a, b, (((ca,), (cb,)), ((), ())),
        precision=lax.Precision.HIGHEST, preferred_element_type=F32,
    )


BF16 = jnp.bfloat16
TERMS = ((2, 0), (0, 2), (1, 1), (1, 0), (0, 1), (0, 0))


def three(a):
    high = a.astype(BF16)
    rest = a - high.astype(F32)
    middle = rest.astype(BF16)
    return high, middle, (rest - middle.astype(F32)).astype(BF16)


def stacked(parts_of, side, axis):
    return jnp.concatenate([p[t[side]] for t in TERMS for p in parts_of], axis=axis)


def spread(v):
    return jnp.broadcast_to(v, (8, HALF))


def eliminate(square, u_ref, li_ref, hook, nb=4):
    sub = lax.broadcasted_iota(jnp.int32, (8, HALF), 0)
    lane = lax.broadcasted_iota(jnp.int32, (8, HALF), 1)
    zero = jnp.zeros((8, HALF), F32)
    tiles = HALF // 8
    left = tuple(square[8 * i : 8 * i + 8, :] for i in range(tiles))
    right = tuple(jnp.where(lane == sub + 8 * i, 1.0, 0.0).astype(F32) for i in range(tiles))

    def eight(left, right, q):
        w = [spread(left[0][:, 8 * q + m : 8 * q + m + 1]) for m in range(8)] + [left[0], right[0]]
        rows = [zero, zero]
        for j in range(0, 8, 2):
            pivot = (sub == j) | (sub == j + 1)
            p00, p01, p11 = spread(w[j][j : j + 1]), spread(w[j][j + 1 : j + 2]), spread(w[j + 1][j + 1 : j + 2])
            rd = 1.0 / (p00 * p11 - p01 * p01)
            i00, i01, i11 = p11 * rd, p01 * rd, p00 * rd
            u, v = jnp.where(pivot, 0.0, w[j]), jnp.where(pivot, 0.0, w[j + 1])
            s0 = lax.rsqrt(p00)
            m0 = p01 * (s0 * s0)
            s1 = lax.rsqrt(p11 - m0 * p01)
            for t in list(range(j + 2, 8)) + [8, 9]:
                r0, r1 = spread(w[t][j : j + 1]), spread(w[t][j + 1 : j + 2])
                a, b = r0 * i00 - r1 * i01, r1 * i11 - r0 * i01
                if t >= 8:
                    rows[t - 8] = jnp.where(
                        sub == j, r0 * s0, jnp.where(sub == j + 1, (r1 - m0 * r0) * s1, rows[t - 8])
                    )
                w[t] = jnp.where(sub == j, a, jnp.where(sub == j + 1, b, w[t] - (u * a + v * b)))
        ql = [spread(w[8][m : m + 1]) for m in range(8)]
        qr = [spread(w[9][m : m + 1]) for m in range(8)]

        def total(c, q):
            t = [c[m] * q[m] for m in range(8)]
            return ((t[0] + t[1]) + (t[2] + t[3])) + ((t[4] + t[5]) + (t[6] + t[7]))

        for i in range(1, tiles):
            c = [spread(left[i][:, 8 * q + m : 8 * q + m + 1]) for m in range(8)]
            left[i] = left[i] - total(c, ql)
            right[i] = right[i] - total(c, qr)
        return rows

    def body(b, carry):
        left, right = list(carry[0]), list(carry[1])
        for q in range(nb):
            up, low = eight(left, right, q)
            r = pl.ds(pl.multiple_of(8 * (b * nb + q), 8), 8)
            up = jnp.where(lane >= sub + 8 * q, up, 0.0)
            u_ref[r, :] = pltpu.roll(up, 8 * nb * b, 1)
            li_ref[r, :] = low
            left, right = left[1:] + [zero], right[1:] + [zero]
        left = [pltpu.roll(t, HALF - 8 * nb, 1) for t in left]
        hook(b)
        return tuple(left), tuple(right)

    lax.fori_loop(0, tiles // nb, body, (left, right))


HEAD, TAIL = slice(0, HALF), slice(HALF, PANEL)


def factor(g_ref, u_ref, li_ref, parts, us, ls, hook):
    parts[0] = g_ref[HEAD, HEAD]

    def block(p, _):
        eliminate(parts[p], us.at[p], ls.at[p], functools.partial(hook, p))

        @pl.when(p == 0)
        def _():
            l11 = ls[0]
            u12 = mm(l11, g_ref[HEAD, TAIL])
            u_ref[HEAD, TAIL] = u12
            parts[1] = g_ref[TAIL, TAIL] - mm(u12, u12, 0, 0)
            li_ref[TAIL, HEAD] = mm(u12, l11, 0, 0)
        return 0

    lax.fori_loop(0, 2, block, 0)
    li_ref[TAIL, HEAD] = -mm(ls[1], li_ref[TAIL, HEAD])
    for p, c in ((0, HEAD), (1, TAIL)):
        u_ref[c, c] = us[p]
        li_ref[c, c] = ls[p]
    u_ref[TAIL, HEAD] = jnp.zeros((HALF, HALF), F32)
    li_ref[HEAD, TAIL] = jnp.zeros((HALF, HALF), F32)


def kernel(scale, a_hbm, out_hbm, upper_ref,
           own, X, S, out, gown, ge, acc, accs, gl, u1, u2, m1, mcat, sq, parts, us, ls,
           ec, ea, eb, lc, la, lb, mc, ma, mb, ly, lx,
           load_sem, out_sem, xs, xr, ss, sr,
           e_core, e_rs, e_y, e_yr, e_ag, e_agc, l_core, l_rs, l_y, l_yr, l_x, l_ag, l_agc, l_agb, l_agbc, m_core, m_rs):
    row, y = lax.axis_index("row"), lax.axis_index("col")
    px, pz, k = row // 8, (row // 2) % 4, row % 2
    qx = px + 1 - 2 * (px % 2)
    across, side = (row, 3 - y), (row, y + 1 - 2 * (y % 2))
    other = (row + 1 - 2 * k, y)

    def on_axis(h, c):
        return (jnp.where(h == 0, (c * 4 + pz) * 2 + k, (px * 4 + c) * 2 + k), y)

    def beside(d):
        return ((qx * 4 + pz) * 2 + k, (y + d) % 4)

    def first(h, x=px):
        return jnp.where(h == 0, x, pz)

    def second(h, x=px):
        return jnp.where(h == 0, pz, x)

    loads = [
        pltpu.make_async_copy(a_hbm.at[pl.ds(1024 * i, 1024)], own.at[pl.ds(1024 * i, 1024)], load_sem.at[i])
        for i in range(4)
    ]
    for c in loads:
        c.start()
    barrier = pltpu.get_barrier_semaphore()
    partners = [across, side, other] + [beside(d) for d in (1, 2, 3)]
    for d in (1, 2, 3):
        partners += [on_axis(0, (px + d) % 4), on_axis(1, (pz + d) % 4)]
    for p in partners:
        pl.semaphore_signal(barrier, inc=1, device_id=p, device_id_type=MESH)
    pl.semaphore_wait(barrier, len(partners))
    for c in loads:
        c.wait()

    def remote(src, dst, send, recv, to):
        return pltpu.make_async_remote_copy(
            src_ref=src, dst_ref=dst, send_sem=send, recv_sem=recv, device_id=to, device_id_type=MESH
        )

    def piece(j):
        return pl.ds(pl.multiple_of(j * CHUNK, CHUNK), CHUNK)

    def to_across(j):
        return remote(own.at[piece(j)], X.at[piece(j)], xs.at[j], xr.at[j], across)

    def to_side(j, src):
        return remote(src.at[piece(j)], S.at[piece(j)], ss.at[j], sr.at[j], side)

    def each(lo, hi, f):
        def step(j, _):
            f(j)
            return 0
        lax.fori_loop(lo, hi, step, 0)

    ahead = 8

    @pl.when(y >= 2)
    def _():
        each(EARLY, EARLY + ahead, lambda j: to_across(j).start())

    def forward(j):
        to_across(j).wait_recv()
        to_side(j, X).start()

        @pl.when(j < EARLY - ahead)
        def _():
            to_across(EARLY + j).wait_send()
            to_across(EARLY + ahead + j).start()

    def turned(j):
        return (j + EARLY) % PIECES

    def sided(j):
        return (y == 0) | (j < EARLY)

    def old_piece(j):
        to_across(j).wait_send()
        pl.when(sided(j))(lambda: to_side(turned(j), own).wait_send())

    def new_piece(j):
        pl.when(j >= LAG)(lambda: old_piece(j - LAG))
        to_across(j).start()
        pl.when(sided(j))(lambda: to_side(turned(j), own).start())

    sent, passed = [0], [0]

    def source(n):
        lo, hi = sent[0], min(sent[0] + n, PIECES)
        sent[0] = hi
        if hi > lo:
            pl.when(y < 2)(lambda: each(lo, hi, new_piece))

    def sink(n):
        lo, hi = passed[0], min(passed[0] + n, PIECES)
        passed[0] = hi
        if hi > lo:
            pl.when(y >= 2)(lambda: each(lo, hi, forward))

    def service(n):
        source(n)
        sink(n)

    def hooked(lo, past):
        def hook(p, b):
            j = 2 * p + b // 2
            pl.when((b % 2 == 1) & (y < 2) & (lo + j < PIECES))(lambda: new_piece(lo + j))
            pl.when((b % 2 == 1) & (y >= 2) & (past + j < PIECES))(lambda: forward(past + j))
        return hook

    base = pl.multiple_of(HALF * k, HALF)

    def lanes(h):
        return pl.ds(pl.multiple_of(HALF * h, HALF), HALF)

    def rows_a(h, c):
        return pl.ds(pl.multiple_of(base + 32 * c, 32), 32)

    def rows_b(h, c, x=px):
        return pl.ds(pl.multiple_of(base + 32 * first(h, x) + 8 * c, 8), 8)

    def exchange(make, n, pause):
        each(0, n, lambda j: make(j).start())
        pause()
        each(0, n, lambda j: make(j).wait())

    def scatter(ref, bc, ba, bb, sem_core, sem_rs):
        def halves(j):
            away = pl.ds(pl.multiple_of(HALF * (1 - k), HALF), HALF)
            return remote(ref.at[:, away], bc, sem_core.at[0], sem_core.at[1], other)

        def wide(j):
            h, d = j // 3, j % 3
            to = (first(h) + d + 1) % 4
            return remote(ref.at[:, rows_a(h, to), lanes(h)], ba.at[h, d],
                          sem_rs.at[0, 0, h, d], sem_rs.at[0, 1, h, d], on_axis(h, to))

        def narrow(j):
            h, d = j // 3, j % 3
            to = (second(h) + d + 1) % 4
            return remote(ref.at[:, rows_b(h, to), lanes(h)], bb.at[h, d],
                          sem_rs.at[1, 0, h, d], sem_rs.at[1, 1, h, d], on_axis(1 - h, to))

        def add_half():
            ref[:, pl.ds(base, HALF), :] += bc[...]

        def add_wide():
            for h in (0, 1):
                ref[:, rows_a(h, first(h)), HALF * h : HALF * h + HALF] += (ba[h, 0] + ba[h, 1]) + ba[h, 2]

        def add_narrow():
            for h in (0, 1):
                ref[:, rows_b(h, second(h)), HALF * h : HALF * h + HALF] += (bb[h, 0] + bb[h, 1]) + bb[h, 2]

        return (halves, 1, add_half), (wide, 6, add_wide), (narrow, 6, add_narrow)

    def begin(stage):
        each(0, stage[1], lambda j: stage[0](j).start())

    def finish(stage):
        each(0, stage[1], lambda j: stage[0](j).wait())
        stage[2]()

    def axis_part(ref, sem_ag, stage):
        def make(j):
            h, d = j // 3, j % 3
            if stage == 0:
                r, axis, coord = rows_b(h, second(h, qx), qx), 1 - h, second(h)
            else:
                r, axis, coord = rows_a(h, first(h, qx)), h, first(h)
            r = ref.at[:, r, lanes(h)]
            return remote(r, r, sem_ag.at[stage, 0, h, d], sem_ag.at[stage, 1, h, d],
                          on_axis(axis, (coord + d + 1) % 4))
        return make

    def core_part(ref, sem_core):
        r = ref.at[:, pl.ds(base, HALF)]
        return lambda j: remote(r, r, sem_core.at[0], sem_core.at[1], other)

    def mine(h, x=px):
        return rows_b(h, second(h, x), x), lanes(h)

    def group(g, ref):
        return ref[pl.ds(pl.multiple_of(g * GROUP, GROUP), GROUP), :]

    source(6)

    @pl.when(y < 2)
    def _():
        gown[...] = jnp.zeros_like(gown)

        def go(g):
            b = group(g, own)
            gown[0] += mm(b, b, 0, 0)
            pl.when(g % 8 == 7)(lambda: new_piece(6 + g // 8))
        each(0, ROWS // GROUP, go)
        sent[0] = 8
        for stage in scatter(gown, ec, ea, eb, e_core, e_rs):
            begin(stage)
            source(1)
            finish(stage)

    acc[...] = jnp.zeros_like(acc)
    accs[...] = jnp.zeros_like(accs)

    def inner(g):
        def two(a, b, c):
            both = mm(jnp.concatenate([group(g, a), group(g, b)], axis=1), group(g, c), 0, 0)
            accs[0] += both[:PANEL]
            accs[1] += both[PANEL:]

        def one(a, b):
            acc[0] += mm(group(g, a), group(g, b), 0, 0)

        @pl.when(y == 0)
        def _():
            two(own, S, X)

        @pl.when(y == 1)
        def _():
            two(S, own, X)
            one(S, own)

        @pl.when(y == 2)
        def _():
            two(S, X, own)

        @pl.when(y == 3)
        def _():
            two(X, S, own)
            one(X, S)

    def shard_send(j):
        h, d = j // 4, j % 4
        return remote(gown.at[(0, *mine(h))], ge.at[(y, *mine(h))], e_y.at[h, d], e_yr.at[y, h], beside(d))

    pl.when(y < 2)(lambda: each(0, 8, lambda j: shard_send(j).start()))
    source(1)
    sink(2)

    def step(i, _):
        @pl.when(y < 2)
        def _():
            new_piece(jnp.where(i == 3, 21, 12 + 2 * i))
            def got(j):
                to_across(j).wait_recv()
                to_side(j, own).wait_recv()

            def tile(t):
                each(2 * t, 2 * t + 2, got)
                inner(t)
            each(8 + 2 * i, 10 + 2 * i, tile)
            pl.when(i < 2)(lambda: new_piece(13 + 2 * i))

        @pl.when(y >= 2)
        def _():
            pl.when(i == 0)(lambda: each(2, 4, forward))
            pl.when(i == 1)(lambda: forward(7))

            def tile(t):
                each(2 * t, 2 * t + 2, lambda j: to_side(j, X).wait_recv())
                inner(t)
            each(2 * i, 2 * i + 2, tile)
            pl.when(i < 2)(lambda: each(4 * i + 4, 4 * i + 6, forward))
            pl.when(i == 2)(lambda: forward(12))

        @pl.when(i == 0)
        def _():
            pl.when(y < 2)(lambda: each(0, 8, lambda j: shard_send(j).wait_send()))

            def got(j):
                src, h = j // 2, j % 2
                v = ge.at[(src, *mine(h, qx))]
                remote(v, v, e_y.at[h, 0], e_yr.at[src, h], beside(0)).wait_recv()
            each(0, 4, got)
            exchange(axis_part(ge, e_ag, 0), 6, lambda: pl.when(y >= 2)(lambda: forward(6)))

        @pl.when(i == 1)
        def _():
            exchange(axis_part(ge, e_ag, 1), 6, lambda: pl.when(y >= 2)(lambda: forward(10)))
            exchange(core_part(ge, e_agc), 1, lambda: pl.when(y >= 2)(lambda: forward(11)))

        @pl.when(i == 2)
        def _():
            ge[...] = ge[...] * scale
            factor(ge.at[0], u1, sq.at[0], parts, us, ls, hooked(17, 13))
        return 0

    lax.fori_loop(0, 4, step, 0)
    sent[0], passed[0] = 22, 17

    lead = scatter(acc, lc, la, lb, l_core, l_rs)
    rest = scatter(accs, mc, ma, mb, m_core, m_rs)
    begin(lead[0])
    begin(rest[0])
    for n, pieces in ((0, 1), (1, 2)):
        service(pieces)
        finish(lead[n])
        begin(lead[n + 1])
        finish(rest[n])
        begin(rest[n + 1])
    service(1)
    finish(lead[2])

    def swap(j):
        h, far = j // 2, j % 2
        r, c = mine(h)
        to = ((qx * 4 + pz) * 2 + k, jnp.where(far == 1, 3 - y, y))
        return remote(accs.at[:, r, c], lx.at[far, h], l_x.at[0, far, h], l_x.at[1, far, h], to)

    def first_send(j):
        h, d = j // 4, j % 4
        return remote(acc.at[(0, *mine(h))], ly.at[y // 2, h], l_y.at[h, d], l_yr.at[y // 2, h], beside(d))

    pl.when(y % 2 == 1)(lambda: each(0, 8, lambda j: first_send(j).start()))
    finish(rest[2])
    each(0, 4, lambda j: swap(j).start())
    service(2)

    def got_first(j):
        src, h = j // 2, j % 2
        v = acc.at[(0, *mine(h))]
        remote(v, ly.at[src, h], l_y.at[h, 0], l_yr.at[src, h], beside(0)).wait_recv()
    each(0, 4, got_first)
    for h in (0, 1):
        r, c = mine(h, qx)
        gl[0, r, c] = ly[0, h] + ly[1, h]
    front, others = gl.at[pl.ds(0, 1)], gl.at[pl.ds(1, 2)]
    near, wide = axis_part(front, l_ag, 0), axis_part(front, l_ag, 1)
    late_near, late_wide = axis_part(others, l_agb, 0), axis_part(others, l_agb, 1)
    late_core = core_part(others, l_agbc)
    each(0, 6, lambda j: near(j).start())
    each(0, 4, lambda j: swap(j).wait())
    for h in (0, 1):
        r, c = mine(h, qx)
        gl[1:3, r, c] = lx[0, h] + lx[1, h]
    each(0, 6, lambda j: late_near(j).start())
    service(1)
    each(0, 6, lambda j: near(j).wait())
    each(0, 6, lambda j: wide(j).start())
    each(0, 6, lambda j: late_near(j).wait())
    each(0, 6, lambda j: late_wide(j).start())
    service(2)
    each(0, 6, lambda j: wide(j).wait())
    exchange(core_part(front, l_agc), 1, lambda: service(1))

    sq[1] = ge[1]
    sq[2] = gl[0] * scale

    def pick(i, a, b, c, d):
        return jnp.where(i == 0, a, jnp.where(i == 1, b, jnp.where(i == 2, c, d)))

    def products(i, _):
        @pl.when(((i == 0) & (y >= 1)) | (y >= 2))
        def _():
            p = mm(sq[pick(i, 0, 0, 5, 6)], sq[pick(i, 2, 3, 10, 11)])
            p = jnp.where(i == 3, sq[7] - p, p)
            sq[pick(i, 6, 7, 8, 12)] = p
            q = mm(sq[pick(i, 6, 6, 5, 0)], p, 0, 0)
            q = jnp.where(i < 2, sq[pick(i, 1, 4, 4, 4)] - q, q)
            sq[pick(i, 9, 10, 11, 13)] = q

        @pl.when(i == 0)
        def _():
            each(0, 6, lambda j: late_wide(j).wait())
            late_core(0).start()
            factor(sq.at[9], u2, sq.at[5], parts, us, ls, hooked(sent[0], passed[0]))
            late_core(0).wait()
            sq[3] = gl[1] * scale
            sq[4] = gl[2] * scale
        return 0

    lax.fori_loop(0, 4, products, 0)
    sent[0], passed[0] = min(sent[0] + 4, PIECES), min(passed[0] + 4, PIECES)
    source(PIECES)

    @pl.when(y == 0)
    def _():
        mcat[: len(TERMS) * PANEL] = stacked([three(sq[0].T)], 1, 0)

    @pl.when(y == 1)
    def _():
        m1[...] = sq[5].T
        m2 = -mm(mm(sq[0], sq[6], 0, 0), m1[...])
        mcat[...] = stacked([three(m1[...]), three(m2)], 1, 0)

    @pl.when(y >= 2)
    def _():
        of_x, of_s = sq[jnp.where(y == 2, 11, 13)], sq[jnp.where(y == 2, 13, 11)]
        mcat[...] = stacked([three(-of_x), three(-of_s)], 1, 0)

    per = APPLY // CHUNK
    steps = ROWS // APPLY

    def part(g):
        return pl.ds(pl.multiple_of(g * APPLY, APPLY), APPLY)

    def store(g):
        return pltpu.make_async_copy(out.at[part(g)], out_hbm.at[part(g)], out_sem.at[g])

    @pl.when(y == 0)
    def _():
        def go(g):
            a = stacked([three(own[part(g), :])], 0, 1)
            out[part(g), :] = jnp.dot(a, mcat[: len(TERMS) * PANEL], preferred_element_type=F32)
            store(g).start()
        each(0, steps, go)

    @pl.when(y == 1)
    def _():
        def go(i):
            g = (i + steps // 2) % steps
            pl.when(g < steps // 2)(lambda: each(per * g, per * g + per, lambda j: to_side(j, own).wait_recv()))
            a = stacked([three(own[part(g), :]), three(S[part(g), :])], 0, 1)
            out[part(g), :] = jnp.dot(a, mcat[...], preferred_element_type=F32)
            store(g).start()
        each(0, steps, go)

    done = passed[0]

    @pl.when(y >= 2)
    def _():
        def reach(g):
            return jnp.minimum(jnp.maximum(done + g, per * g + per), PIECES)
        def go(g):
            each(jnp.where(g == 0, done, reach(g - 1)), reach(g), forward)
            pl.when(g >= steps // 2)(lambda: each(per * g, per * g + per, lambda j: to_side(j, X).wait_recv()))
            a = stacked([three(X[part(g), :]), three(S[part(g), :])], 0, 1)
            out[part(g), :] = own[part(g), :] + jnp.dot(a, mcat[...], preferred_element_type=F32)
            store(g).start()
        each(0, steps, go)

    @pl.when(y == 0)
    def _():
        upper_ref[:PANEL] = u1[...]
        upper_ref[PANEL:] = jnp.zeros((PANEL, PANEL), F32)

    @pl.when(y == 1)
    def _():
        upper_ref[:PANEL] = sq[6]
        upper_ref[PANEL:] = u2[...]

    @pl.when(y >= 2)
    def _():
        upper_ref[:PANEL] = sq[7]
        upper_ref[PANEL:] = sq[8]

    pl.when(y % 2 == 1)(lambda: each(0, 8, lambda j: first_send(j).wait_send()))

    @pl.when(y < 2)
    def _():
        each(PIECES - LAG, PIECES, old_piece)

    @pl.when(y >= 2)
    def _():
        each(PIECES - ahead, PIECES, lambda j: to_across(j).wait_send())
        each(0, PIECES, lambda j: to_side(j, X).wait_send())

    each(0, steps, lambda g: store(g).wait())


PLACED = 4


def place(a_ref, b_ref, out_ref, upper_ref, a_buf, b_buf, sems):
    step = ROWS // PLACED
    pairs = [(a_ref.at[pl.ds(i * step, step)], a_buf.at[pl.ds(i * step, step)], out_ref.at[pl.ds(i * step, step)])
             for i in range(PLACED)] + [(b_ref, b_buf, upper_ref)]
    ins = [pltpu.make_async_copy(s, b, sems.at[0, i]) for i, (s, b, _) in enumerate(pairs)]
    outs = [pltpu.make_async_copy(b, d, sems.at[1, i]) for i, (_, b, d) in enumerate(pairs)]
    for c in ins:
        c.start()
    for c, d in zip(ins, outs):
        c.wait()
        d.start()
    for d in outs:
        d.wait()


def on_device(total_rows, influence):
    vmem = lambda *s: pltpu.VMEM(s, F32)
    dma = lambda *s: pltpu.SemaphoreType.DMA(s)
    block = vmem(PANEL, PANEL)
    factored, upper = pl.pallas_call(
        functools.partial(kernel, 1.0 / total_rows),
        name="factor_panels",
        out_shape=[jax.ShapeDtypeStruct((ROWS, PANEL), F32), jax.ShapeDtypeStruct((2 * PANEL, PANEL), F32)],
        in_specs=[pl.BlockSpec(memory_space=pl.ANY)],
        out_specs=[pl.BlockSpec(memory_space=pl.ANY)] + [pl.BlockSpec(memory_space=pltpu.VMEM)],
        scratch_shapes=[
            vmem(ROWS, PANEL), vmem(ROWS, PANEL), vmem(ROWS, PANEL), vmem(ROWS, PANEL),
            vmem(1, PANEL, PANEL), vmem(2, PANEL, PANEL), vmem(1, PANEL, PANEL), vmem(2, PANEL, PANEL),
            vmem(3, PANEL, PANEL),
            block, block, block, pltpu.VMEM((2 * len(TERMS) * PANEL, PANEL), BF16), vmem(14, PANEL, PANEL),
            vmem(2, HALF, HALF), vmem(2, HALF, HALF), vmem(2, HALF, HALF),
            vmem(1, HALF, PANEL), vmem(2, 3, 1, 32, HALF), vmem(2, 3, 1, 8, HALF),
            vmem(1, HALF, PANEL), vmem(2, 3, 1, 32, HALF), vmem(2, 3, 1, 8, HALF),
            vmem(2, HALF, PANEL), vmem(2, 3, 2, 32, HALF), vmem(2, 3, 2, 8, HALF),
            vmem(2, 2, 8, HALF), vmem(2, 2, 2, 8, HALF),
            dma(4), dma(ROWS // APPLY), dma(PIECES), dma(PIECES), dma(PIECES), dma(PIECES),
            dma(2), dma(2, 2, 2, 3), dma(2, 4), dma(2, 2), dma(2, 2, 2, 3), dma(2),
            dma(2), dma(2, 2, 2, 3), dma(2, 4), dma(2, 2), dma(2, 2, 2), dma(2, 2, 2, 3), dma(2),
            dma(2, 2, 2, 3), dma(2), dma(2), dma(2, 2, 2, 3),
        ],
        compiler_params=pltpu.CompilerParams(
            collective_id=0, has_side_effects=True, vmem_limit_bytes=56 * 2**20
        ),
    )(influence)
    return pl.pallas_call(
        place,
        name="place_results",
        out_shape=[jax.ShapeDtypeStruct((ROWS, PANEL), F32), jax.ShapeDtypeStruct((2 * PANEL, PANEL), F32)],
        in_specs=[pl.BlockSpec(memory_space=pl.ANY)] * 2,
        out_specs=[pl.BlockSpec(memory_space=pl.ANY)] * 2,
        scratch_shapes=[vmem(ROWS, PANEL), vmem(2 * PANEL, PANEL), dma(2, PLACED + 1)],
        compiler_params=pltpu.CompilerParams(vmem_limit_bytes=60 * 2**20),
    )(factored, upper)


def solution(mesh):
    total_rows = ROWS * mesh.shape["row"]
    return jax.shard_map(
        functools.partial(on_device, total_rows),
        mesh=mesh,
        in_specs=(P("row", "col"),),
        out_specs=(P("row", "col"), P(None, "col")),
        check_vma=False,
    )
```

```python
import functools

import jax
import jax.numpy as jnp
from jax import lax
from jax.experimental import pallas as pl
from jax.experimental.pallas import tpu as pltpu
from jax.sharding import PartitionSpec as P

MESH = pl.DeviceIdType.MESH
F32 = jnp.float32
PANEL = 256
HALF = 128
ROWS = 4096
CHUNK = 128
PIECES = ROWS // CHUNK
EARLY = PIECES // 2
GROUP = 256
LAG = 6
APPLY = 512


def mm(a, b, ca=1, cb=0):
    return lax.dot_general(
        a, b, (((ca,), (cb,)), ((), ())),
        precision=lax.Precision.HIGHEST, preferred_element_type=F32,
    )


BF16 = jnp.bfloat16
TERMS = ((2, 0), (0, 2), (1, 1), (1, 0), (0, 1), (0, 0))


def three(a):
    high = a.astype(BF16)
    rest = a - high.astype(F32)
    middle = rest.astype(BF16)
    return high, middle, (rest - middle.astype(F32)).astype(BF16)


def stacked(parts_of, side, axis):
    return jnp.concatenate([p[t[side]] for t in TERMS for p in parts_of], axis=axis)


def spread(v):
    return jnp.broadcast_to(v, (8, HALF))


def eliminate(square, u_ref, li_ref, hook, nb=4):
    sub = lax.broadcasted_iota(jnp.int32, (8, HALF), 0)
    lane = lax.broadcasted_iota(jnp.int32, (8, HALF), 1)
    zero = jnp.zeros((8, HALF), F32)
    tiles = HALF // 8
    left = tuple(square[8 * i : 8 * i + 8, :] for i in range(tiles))
    right = tuple(jnp.where(lane == sub + 8 * i, 1.0, 0.0).astype(F32) for i in range(tiles))

    def eight(left, right, q):
        w = [spread(left[0][:, 8 * q + m : 8 * q + m + 1]) for m in range(8)] + [left[0], right[0]]
        rows = [zero, zero]
        for j in range(0, 8, 2):
            pivot = (sub == j) | (sub == j + 1)
            p00, p01, p11 = spread(w[j][j : j + 1]), spread(w[j][j + 1 : j + 2]), spread(w[j + 1][j + 1 : j + 2])
            rd = 1.0 / (p00 * p11 - p01 * p01)
            i00, i01, i11 = p11 * rd, p01 * rd, p00 * rd
            u, v = jnp.where(pivot, 0.0, w[j]), jnp.where(pivot, 0.0, w[j + 1])
            s0 = lax.rsqrt(p00)
            m0 = p01 * (s0 * s0)
            s1 = lax.rsqrt(p11 - m0 * p01)
            for t in list(range(j + 2, 8)) + [8, 9]:
                r0, r1 = spread(w[t][j : j + 1]), spread(w[t][j + 1 : j + 2])
                a, b = r0 * i00 - r1 * i01, r1 * i11 - r0 * i01
                if t >= 8:
                    rows[t - 8] = jnp.where(
                        sub == j, r0 * s0, jnp.where(sub == j + 1, (r1 - m0 * r0) * s1, rows[t - 8])
                    )
                w[t] = jnp.where(sub == j, a, jnp.where(sub == j + 1, b, w[t] - (u * a + v * b)))
        ql = [spread(w[8][m : m + 1]) for m in range(8)]
        qr = [spread(w[9][m : m + 1]) for m in range(8)]

        def total(c, q):
            t = [c[m] * q[m] for m in range(8)]
            return ((t[0] + t[1]) + (t[2] + t[3])) + ((t[4] + t[5]) + (t[6] + t[7]))

        for i in range(1, tiles):
            c = [spread(left[i][:, 8 * q + m : 8 * q + m + 1]) for m in range(8)]
            left[i] = left[i] - total(c, ql)
            right[i] = right[i] - total(c, qr)
        return rows

    def body(b, carry):
        left, right = list(carry[0]), list(carry[1])
        for q in range(nb):
            up, low = eight(left, right, q)
            r = pl.ds(pl.multiple_of(8 * (b * nb + q), 8), 8)
            up = jnp.where(lane >= sub + 8 * q, up, 0.0)
            u_ref[r, :] = pltpu.roll(up, 8 * nb * b, 1)
            li_ref[r, :] = low
            left, right = left[1:] + [zero], right[1:] + [zero]
        left = [pltpu.roll(t, HALF - 8 * nb, 1) for t in left]
        hook(b)
        return tuple(left), tuple(right)

    lax.fori_loop(0, tiles // nb, body, (left, right))


HEAD, TAIL = slice(0, HALF), slice(HALF, PANEL)


def factor(g_ref, u_ref, li_ref, parts, us, ls, hook):
    parts[0] = g_ref[HEAD, HEAD]

    def block(p, _):
        eliminate(parts[p], us.at[p], ls.at[p], functools.partial(hook, p))

        @pl.when(p == 0)
        def _():
            l11 = ls[0]
            u12 = mm(l11, g_ref[HEAD, TAIL])
            u_ref[HEAD, TAIL] = u12
            parts[1] = g_ref[TAIL, TAIL] - mm(u12, u12, 0, 0)
            li_ref[TAIL, HEAD] = mm(u12, l11, 0, 0)
        return 0

    lax.fori_loop(0, 2, block, 0)
    li_ref[TAIL, HEAD] = -mm(ls[1], li_ref[TAIL, HEAD])
    for p, c in ((0, HEAD), (1, TAIL)):
        u_ref[c, c] = us[p]
        li_ref[c, c] = ls[p]
    u_ref[TAIL, HEAD] = jnp.zeros((HALF, HALF), F32)
    li_ref[HEAD, TAIL] = jnp.zeros((HALF, HALF), F32)


def kernel(scale, a_hbm, out_hbm, upper_hbm,
           own, X, S, out, gown, ge, acc, accs, gl, u1, u2, m1, mcat, sq, parts, us, ls,
           ec, ea, eb, lc, la, lb, mc, ma, mb, ly, lx,
           load_sem, out_sem, xs, xr, ss, sr,
           e_core, e_rs, e_y, e_yr, e_ag, e_agc, l_core, l_rs, l_y, l_yr, l_x, l_ag, l_agc, l_agb, l_agbc, m_core, m_rs, up_sem):
    row, y = lax.axis_index("row"), lax.axis_index("col")
    px, pz, k = row // 8, (row // 2) % 4, row % 2
    qx = px + 1 - 2 * (px % 2)
    across, side = (row, 3 - y), (row, y + 1 - 2 * (y % 2))
    other = (row + 1 - 2 * k, y)

    def on_axis(h, c):
        return (jnp.where(h == 0, (c * 4 + pz) * 2 + k, (px * 4 + c) * 2 + k), y)

    def beside(d):
        return ((qx * 4 + pz) * 2 + k, (y + d) % 4)

    def first(h, x=px):
        return jnp.where(h == 0, x, pz)

    def second(h, x=px):
        return jnp.where(h == 0, pz, x)

    loads = [
        pltpu.make_async_copy(a_hbm.at[pl.ds(1024 * i, 1024)], own.at[pl.ds(1024 * i, 1024)], load_sem.at[i])
        for i in range(4)
    ]
    for c in loads:
        c.start()
    barrier = pltpu.get_barrier_semaphore()
    partners = [across, side, other] + [beside(d) for d in (1, 2, 3)]
    for d in (1, 2, 3):
        partners += [on_axis(0, (px + d) % 4), on_axis(1, (pz + d) % 4)]
    for p in partners:
        pl.semaphore_signal(barrier, inc=1, device_id=p, device_id_type=MESH)
    pl.semaphore_wait(barrier, len(partners))
    for c in loads:
        c.wait()

    def remote(src, dst, send, recv, to):
        return pltpu.make_async_remote_copy(
            src_ref=src, dst_ref=dst, send_sem=send, recv_sem=recv, device_id=to, device_id_type=MESH
        )

    def piece(j):
        return pl.ds(pl.multiple_of(j * CHUNK, CHUNK), CHUNK)

    def to_across(j):
        return remote(own.at[piece(j)], X.at[piece(j)], xs.at[j], xr.at[j], across)

    def to_side(j, src):
        return remote(src.at[piece(j)], S.at[piece(j)], ss.at[j], sr.at[j], side)

    def each(lo, hi, f):
        def step(j, _):
            f(j)
            return 0
        lax.fori_loop(lo, hi, step, 0)

    ahead = 8

    @pl.when(y >= 2)
    def _():
        each(EARLY, EARLY + ahead, lambda j: to_across(j).start())

    def forward(j):
        to_across(j).wait_recv()
        to_side(j, X).start()

        @pl.when(j < EARLY - ahead)
        def _():
            to_across(EARLY + j).wait_send()
            to_across(EARLY + ahead + j).start()

    def turned(j):
        return (j + EARLY) % PIECES

    def sided(j):
        return (y == 0) | (j < EARLY)

    def old_piece(j):
        to_across(j).wait_send()
        pl.when(sided(j))(lambda: to_side(turned(j), own).wait_send())

    def new_piece(j):
        pl.when(j >= LAG)(lambda: old_piece(j - LAG))
        to_across(j).start()
        pl.when(sided(j))(lambda: to_side(turned(j), own).start())

    sent, passed = [0], [0]

    def source(n):
        lo, hi = sent[0], min(sent[0] + n, PIECES)
        sent[0] = hi
        if hi > lo:
            pl.when(y < 2)(lambda: each(lo, hi, new_piece))

    def sink(n):
        lo, hi = passed[0], min(passed[0] + n, PIECES)
        passed[0] = hi
        if hi > lo:
            pl.when(y >= 2)(lambda: each(lo, hi, forward))

    def service(n):
        source(n)
        sink(n)

    def hooked(lo, past):
        def hook(p, b):
            j = 2 * p + b // 2
            pl.when((b % 2 == 1) & (y < 2) & (lo + j < PIECES))(lambda: new_piece(lo + j))
            pl.when((b % 2 == 1) & (y >= 2) & (past + j < PIECES))(lambda: forward(past + j))
        return hook

    base = pl.multiple_of(HALF * k, HALF)

    def lanes(h):
        return pl.ds(pl.multiple_of(HALF * h, HALF), HALF)

    def rows_a(h, c):
        return pl.ds(pl.multiple_of(base + 32 * c, 32), 32)

    def rows_b(h, c, x=px):
        return pl.ds(pl.multiple_of(base + 32 * first(h, x) + 8 * c, 8), 8)

    def exchange(make, n, pause):
        each(0, n, lambda j: make(j).start())
        pause()
        each(0, n, lambda j: make(j).wait())

    def scatter(ref, bc, ba, bb, sem_core, sem_rs):
        def halves(j):
            away = pl.ds(pl.multiple_of(HALF * (1 - k), HALF), HALF)
            return remote(ref.at[:, away], bc, sem_core.at[0], sem_core.at[1], other)

        def wide(j):
            h, d = j // 3, j % 3
            to = (first(h) + d + 1) % 4
            return remote(ref.at[:, rows_a(h, to), lanes(h)], ba.at[h, d],
                          sem_rs.at[0, 0, h, d], sem_rs.at[0, 1, h, d], on_axis(h, to))

        def narrow(j):
            h, d = j // 3, j % 3
            to = (second(h) + d + 1) % 4
            return remote(ref.at[:, rows_b(h, to), lanes(h)], bb.at[h, d],
                          sem_rs.at[1, 0, h, d], sem_rs.at[1, 1, h, d], on_axis(1 - h, to))

        def add_half():
            ref[:, pl.ds(base, HALF), :] += bc[...]

        def add_wide():
            for h in (0, 1):
                ref[:, rows_a(h, first(h)), HALF * h : HALF * h + HALF] += (ba[h, 0] + ba[h, 1]) + ba[h, 2]

        def add_narrow():
            for h in (0, 1):
                ref[:, rows_b(h, second(h)), HALF * h : HALF * h + HALF] += (bb[h, 0] + bb[h, 1]) + bb[h, 2]

        return (halves, 1, add_half), (wide, 6, add_wide), (narrow, 6, add_narrow)

    def begin(stage):
        each(0, stage[1], lambda j: stage[0](j).start())

    def finish(stage):
        each(0, stage[1], lambda j: stage[0](j).wait())
        stage[2]()

    def axis_part(ref, sem_ag, stage):
        def make(j):
            h, d = j // 3, j % 3
            if stage == 0:
                r, axis, coord = rows_b(h, second(h, qx), qx), 1 - h, second(h)
            else:
                r, axis, coord = rows_a(h, first(h, qx)), h, first(h)
            r = ref.at[:, r, lanes(h)]
            return remote(r, r, sem_ag.at[stage, 0, h, d], sem_ag.at[stage, 1, h, d],
                          on_axis(axis, (coord + d + 1) % 4))
        return make

    def core_part(ref, sem_core):
        r = ref.at[:, pl.ds(base, HALF)]
        return lambda j: remote(r, r, sem_core.at[0], sem_core.at[1], other)

    def mine(h, x=px):
        return rows_b(h, second(h, x), x), lanes(h)

    def group(g, ref):
        return ref[pl.ds(pl.multiple_of(g * GROUP, GROUP), GROUP), :]

    source(6)

    @pl.when(y < 2)
    def _():
        gown[...] = jnp.zeros_like(gown)

        def go(g):
            b = group(g, own)
            gown[0] += mm(b, b, 0, 0)
            pl.when(g % 8 == 7)(lambda: new_piece(6 + g // 8))
        each(0, ROWS // GROUP, go)
        sent[0] = 8
        for stage in scatter(gown, ec, ea, eb, e_core, e_rs):
            begin(stage)
            source(1)
            finish(stage)

    acc[...] = jnp.zeros_like(acc)
    accs[...] = jnp.zeros_like(accs)

    def inner(g):
        def two(a, b, c):
            both = mm(jnp.concatenate([group(g, a), group(g, b)], axis=1), group(g, c), 0, 0)
            accs[0] += both[:PANEL]
            accs[1] += both[PANEL:]

        def one(a, b):
            acc[0] += mm(group(g, a), group(g, b), 0, 0)

        @pl.when(y == 0)
        def _():
            two(own, S, X)

        @pl.when(y == 1)
        def _():
            two(S, own, X)
            one(S, own)

        @pl.when(y == 2)
        def _():
            two(S, X, own)

        @pl.when(y == 3)
        def _():
            two(X, S, own)
            one(X, S)

    def shard_send(j):
        h, d = j // 4, j % 4
        return remote(gown.at[(0, *mine(h))], ge.at[(y, *mine(h))], e_y.at[h, d], e_yr.at[y, h], beside(d))

    pl.when(y < 2)(lambda: each(0, 8, lambda j: shard_send(j).start()))
    source(1)
    sink(2)

    def step(i, _):
        @pl.when(y < 2)
        def _():
            new_piece(jnp.where(i == 3, 21, 12 + 2 * i))
            def got(j):
                to_across(j).wait_recv()
                to_side(j, own).wait_recv()

            def tile(t):
                each(2 * t, 2 * t + 2, got)
                inner(t)
            each(8 + 2 * i, 10 + 2 * i, tile)
            pl.when(i < 2)(lambda: new_piece(13 + 2 * i))

        @pl.when(y >= 2)
        def _():
            pl.when(i == 0)(lambda: each(2, 4, forward))
            pl.when(i == 1)(lambda: forward(7))

            def tile(t):
                each(2 * t, 2 * t + 2, lambda j: to_side(j, X).wait_recv())
                inner(t)
            each(2 * i, 2 * i + 2, tile)
            pl.when(i < 2)(lambda: each(4 * i + 4, 4 * i + 6, forward))
            pl.when(i == 2)(lambda: forward(12))

        @pl.when(i == 0)
        def _():
            pl.when(y < 2)(lambda: each(0, 8, lambda j: shard_send(j).wait_send()))

            def got(j):
                src, h = j // 2, j % 2
                v = ge.at[(src, *mine(h, qx))]
                remote(v, v, e_y.at[h, 0], e_yr.at[src, h], beside(0)).wait_recv()
            each(0, 4, got)
            exchange(axis_part(ge, e_ag, 0), 6, lambda: pl.when(y >= 2)(lambda: forward(6)))

        @pl.when(i == 1)
        def _():
            exchange(axis_part(ge, e_ag, 1), 6, lambda: pl.when(y >= 2)(lambda: forward(10)))
            exchange(core_part(ge, e_agc), 1, lambda: pl.when(y >= 2)(lambda: forward(11)))

        @pl.when(i == 2)
        def _():
            ge[...] = ge[...] * scale
            factor(ge.at[0], u1, sq.at[0], parts, us, ls, hooked(17, 13))
        return 0

    lax.fori_loop(0, 4, step, 0)
    sent[0], passed[0] = 22, 17

    lead = scatter(acc, lc, la, lb, l_core, l_rs)
    rest = scatter(accs, mc, ma, mb, m_core, m_rs)
    begin(lead[0])
    begin(rest[0])
    for n, pieces in ((0, 1), (1, 2)):
        service(pieces)
        finish(lead[n])
        begin(lead[n + 1])
        finish(rest[n])
        begin(rest[n + 1])
    service(1)
    finish(lead[2])

    def swap(j):
        h, far = j // 2, j % 2
        r, c = mine(h)
        to = ((qx * 4 + pz) * 2 + k, jnp.where(far == 1, 3 - y, y))
        return remote(accs.at[:, r, c], lx.at[far, h], l_x.at[0, far, h], l_x.at[1, far, h], to)

    def first_send(j):
        h, d = j // 4, j % 4
        return remote(acc.at[(0, *mine(h))], ly.at[y // 2, h], l_y.at[h, d], l_yr.at[y // 2, h], beside(d))

    pl.when(y % 2 == 1)(lambda: each(0, 8, lambda j: first_send(j).start()))
    finish(rest[2])
    each(0, 4, lambda j: swap(j).start())
    service(2)

    def got_first(j):
        src, h = j // 2, j % 2
        v = acc.at[(0, *mine(h))]
        remote(v, ly.at[src, h], l_y.at[h, 0], l_yr.at[src, h], beside(0)).wait_recv()
    each(0, 4, got_first)
    for h in (0, 1):
        r, c = mine(h, qx)
        gl[0, r, c] = ly[0, h] + ly[1, h]
    front, others = gl.at[pl.ds(0, 1)], gl.at[pl.ds(1, 2)]
    near, wide = axis_part(front, l_ag, 0), axis_part(front, l_ag, 1)
    late_near, late_wide = axis_part(others, l_agb, 0), axis_part(others, l_agb, 1)
    late_core = core_part(others, l_agbc)
    each(0, 6, lambda j: near(j).start())
    each(0, 4, lambda j: swap(j).wait())
    for h in (0, 1):
        r, c = mine(h, qx)
        gl[1:3, r, c] = lx[0, h] + lx[1, h]
    each(0, 6, lambda j: late_near(j).start())
    service(1)
    each(0, 6, lambda j: near(j).wait())
    each(0, 6, lambda j: wide(j).start())
    each(0, 6, lambda j: late_near(j).wait())
    each(0, 6, lambda j: late_wide(j).start())
    service(2)
    each(0, 6, lambda j: wide(j).wait())
    exchange(core_part(front, l_agc), 1, lambda: service(1))

    sq[1] = ge[1]
    sq[2] = gl[0] * scale

    def pick(i, a, b, c, d):
        return jnp.where(i == 0, a, jnp.where(i == 1, b, jnp.where(i == 2, c, d)))

    def products(i, _):
        @pl.when(((i == 0) & (y >= 1)) | (y >= 2))
        def _():
            p = mm(sq[pick(i, 0, 0, 5, 6)], sq[pick(i, 2, 3, 10, 11)])
            p = jnp.where(i == 3, sq[7] - p, p)
            sq[pick(i, 6, 7, 8, 12)] = p
            q = mm(sq[pick(i, 6, 6, 5, 0)], p, 0, 0)
            q = jnp.where(i < 2, sq[pick(i, 1, 4, 4, 4)] - q, q)
            sq[pick(i, 9, 10, 11, 13)] = q

        @pl.when(i == 0)
        def _():
            each(0, 6, lambda j: late_wide(j).wait())
            late_core(0).start()
            factor(sq.at[9], u2, sq.at[5], parts, us, ls, hooked(sent[0], passed[0]))
            late_core(0).wait()
            sq[3] = gl[1] * scale
            sq[4] = gl[2] * scale
        return 0

    lax.fori_loop(0, 4, products, 0)
    sent[0], passed[0] = min(sent[0] + 4, PIECES), min(passed[0] + 4, PIECES)
    source(PIECES)

    @pl.when(y == 0)
    def _():
        mcat[: len(TERMS) * PANEL] = stacked([three(sq[0].T)], 1, 0)

    @pl.when(y == 1)
    def _():
        m1[...] = sq[5].T
        m2 = -mm(mm(sq[0], sq[6], 0, 0), m1[...])
        mcat[...] = stacked([three(m1[...]), three(m2)], 1, 0)

    @pl.when(y >= 2)
    def _():
        of_x, of_s = sq[jnp.where(y == 2, 11, 13)], sq[jnp.where(y == 2, 13, 11)]
        mcat[...] = stacked([three(-of_x), three(-of_s)], 1, 0)

    pl.when(y == 0)(lambda: sq.__setitem__(8, jnp.zeros((PANEL, PANEL), F32)))

    def uppers(do):
        def both(top, bottom):
            do(pltpu.make_async_copy(top, upper_hbm.at[pl.ds(0, PANEL)], up_sem.at[0]))
            do(pltpu.make_async_copy(bottom, upper_hbm.at[pl.ds(PANEL, PANEL)], up_sem.at[1]))
        pl.when(y == 0)(lambda: both(u1, sq.at[8]))
        pl.when(y == 1)(lambda: both(sq.at[6], u2))
        pl.when(y >= 2)(lambda: both(sq.at[7], sq.at[8]))

    uppers(lambda c: c.start())

    per = APPLY // CHUNK
    steps = ROWS // APPLY

    def part(g):
        return pl.ds(pl.multiple_of(g * APPLY, APPLY), APPLY)

    def store(g):
        return pltpu.make_async_copy(out.at[part(g)], out_hbm.at[part(g)], out_sem.at[g])

    @pl.when(y == 0)
    def _():
        def go(g):
            a = stacked([three(own[part(g), :])], 0, 1)
            out[part(g), :] = jnp.dot(a, mcat[: len(TERMS) * PANEL], preferred_element_type=F32)
            store(g).start()
        each(0, steps, go)

    @pl.when(y == 1)
    def _():
        def go(i):
            g = (i + steps // 2) % steps
            pl.when(g < steps // 2)(lambda: each(per * g, per * g + per, lambda j: to_side(j, own).wait_recv()))
            a = stacked([three(own[part(g), :]), three(S[part(g), :])], 0, 1)
            out[part(g), :] = jnp.dot(a, mcat[...], preferred_element_type=F32)
            store(g).start()
        each(0, steps, go)

    done = passed[0]

    @pl.when(y >= 2)
    def _():
        def reach(g):
            return jnp.minimum(jnp.maximum(done + g, per * g + per), PIECES)
        def go(g):
            each(jnp.where(g == 0, done, reach(g - 1)), reach(g), forward)
            pl.when(g >= steps // 2)(lambda: each(per * g, per * g + per, lambda j: to_side(j, X).wait_recv()))
            a = stacked([three(X[part(g), :]), three(S[part(g), :])], 0, 1)
            out[part(g), :] = own[part(g), :] + jnp.dot(a, mcat[...], preferred_element_type=F32)
            store(g).start()
        each(0, steps, go)

    uppers(lambda c: c.wait())
    pl.when(y % 2 == 1)(lambda: each(0, 8, lambda j: first_send(j).wait_send()))

    @pl.when(y < 2)
    def _():
        each(PIECES - LAG, PIECES, old_piece)

    @pl.when(y >= 2)
    def _():
        each(PIECES - ahead, PIECES, lambda j: to_across(j).wait_send())
        each(0, PIECES, lambda j: to_side(j, X).wait_send())

    each(0, steps, lambda g: store(g).wait())


PLACED = 4


def place(a_ref, b_ref, out_ref, upper_ref, a_buf, b_buf, sems):
    step = ROWS // PLACED
    pairs = [(a_ref.at[pl.ds(i * step, step)], a_buf.at[pl.ds(i * step, step)], out_ref.at[pl.ds(i * step, step)])
             for i in range(PLACED)] + [(b_ref, b_buf, upper_ref)]
    ins = [pltpu.make_async_copy(s, b, sems.at[0, i]) for i, (s, b, _) in enumerate(pairs)]
    outs = [pltpu.make_async_copy(b, d, sems.at[1, i]) for i, (_, b, d) in enumerate(pairs)]
    for c in ins:
        c.start()
    for c, d in zip(ins, outs):
        c.wait()
        d.start()
    for d in outs:
        d.wait()


def on_device(total_rows, influence):
    vmem = lambda *s: pltpu.VMEM(s, F32)
    dma = lambda *s: pltpu.SemaphoreType.DMA(s)
    block = vmem(PANEL, PANEL)
    factored, upper = pl.pallas_call(
        functools.partial(kernel, 1.0 / total_rows),
        name="factor_panels",
        out_shape=[jax.ShapeDtypeStruct((ROWS, PANEL), F32), jax.ShapeDtypeStruct((2 * PANEL, PANEL), F32)],
        in_specs=[pl.BlockSpec(memory_space=pl.ANY)],
        out_specs=[pl.BlockSpec(memory_space=pl.ANY)] * 2,
        scratch_shapes=[
            vmem(ROWS, PANEL), vmem(ROWS, PANEL), vmem(ROWS, PANEL), vmem(ROWS, PANEL),
            vmem(1, PANEL, PANEL), vmem(2, PANEL, PANEL), vmem(1, PANEL, PANEL), vmem(2, PANEL, PANEL),
            vmem(3, PANEL, PANEL),
            block, block, block, pltpu.VMEM((2 * len(TERMS) * PANEL, PANEL), BF16), vmem(14, PANEL, PANEL),
            vmem(2, HALF, HALF), vmem(2, HALF, HALF), vmem(2, HALF, HALF),
            vmem(1, HALF, PANEL), vmem(2, 3, 1, 32, HALF), vmem(2, 3, 1, 8, HALF),
            vmem(1, HALF, PANEL), vmem(2, 3, 1, 32, HALF), vmem(2, 3, 1, 8, HALF),
            vmem(2, HALF, PANEL), vmem(2, 3, 2, 32, HALF), vmem(2, 3, 2, 8, HALF),
            vmem(2, 2, 8, HALF), vmem(2, 2, 2, 8, HALF),
            dma(4), dma(ROWS // APPLY), dma(PIECES), dma(PIECES), dma(PIECES), dma(PIECES),
            dma(2), dma(2, 2, 2, 3), dma(2, 4), dma(2, 2), dma(2, 2, 2, 3), dma(2),
            dma(2), dma(2, 2, 2, 3), dma(2, 4), dma(2, 2), dma(2, 2, 2), dma(2, 2, 2, 3), dma(2),
            dma(2, 2, 2, 3), dma(2), dma(2), dma(2, 2, 2, 3), dma(2),
        ],
        compiler_params=pltpu.CompilerParams(
            collective_id=0, has_side_effects=True, vmem_limit_bytes=56 * 2**20
        ),
    )(influence)
    return pl.pallas_call(
        place,
        name="place_results",
        out_shape=[jax.ShapeDtypeStruct((ROWS, PANEL), F32), jax.ShapeDtypeStruct((2 * PANEL, PANEL), F32)],
        in_specs=[pl.BlockSpec(memory_space=pl.ANY)] * 2,
        out_specs=[pl.BlockSpec(memory_space=pl.ANY)] * 2,
        scratch_shapes=[vmem(ROWS, PANEL), vmem(2 * PANEL, PANEL), dma(2, PLACED + 1)],
        compiler_params=pltpu.CompilerParams(vmem_limit_bytes=60 * 2**20),
    )(factored, upper)


def solution(mesh):
    total_rows = ROWS * mesh.shape["row"]
    return jax.shard_map(
        functools.partial(on_device, total_rows),
        mesh=mesh,
        in_specs=(P("row", "col"),),
        out_specs=(P("row", "col"), P(None, "col")),
        check_vma=False,
    )
```
